128 devices in a mesh: rad: 4 (over z_lo, core), phi: 32 (over x, y, z_hi).
Axes of the slice: x: 4, y: 4, z: 4 (z_hi: 2, z_lo: 2; z = z_hi * 2 + z_lo), core: 2. Of those that a mesh axis runs over, the one named last changes fastest.
Arguments:
- density: float32 [2, 512, 16384], P(None, 'rad', 'phi'), may hold values from 0.5 to 2
- carried: float32 [7, 2, 512, 16384], P(None, None, 'rad', 'phi'), may hold values from -1.5 to 1.5
- cycle_shift: int32 [512], P('rad'), may hold values from 0 to 16383
- cycle_fraction: float32 [512], P('rad'), may hold values from 0 to 1
Outputs:
- density_next: float32 [2, 512, 16384], P(None, 'rad', 'phi')
- carried_next: float32 [7, 2, 512, 16384], P(None, None, 'rad', 'phi')
The draws below stay inside these ranges and needn't reach their ends.
All inputs are finite; a program needn't handle non-finite values.
Results may differ from the reference program's by a relative error of at most 0.00002.
Values sent between devices are 32-bit elements; how exact they have to be, the bound alone decides.
No kernel may reach another device: no remote copies, remote signals or barrier semaphores. Data moves between devices by JAX's collectives and lax.ppermute only.
A program may use at most 192 MiB of HBM per device.

```python
import math
import jax
import jax.numpy as jnp

Z = 2
NR = 512
NPHI = 16384


def plant(drawn, key, low, largest):
    longest = drawn.shape.index(max(drawn.shape))
    spots = []
    for shift in (0, 1):
        where = [jax.random.randint(jax.random.fold_in(key, axis), (), 0, length) for axis, length in enumerate(drawn.shape)]
        where[longest] = (where[longest] + shift) % drawn.shape[longest]
        spots.append(tuple(where))
    return drawn.at[spots[0]].set(low).at[spots[1]].set(largest)


def shard_levels(rng, dims, split, least, high):
    level = 1.0
    for dim, parts in split:
        steps = jax.random.uniform(jax.random.fold_in(jax.random.fold_in(rng, 6), dim), (parts,), jnp.float32, least / len(split), high / len(split))
        level = level * jnp.repeat(jnp.exp(steps), dims[dim] // parts).reshape((-1,) + (1,) * (len(dims) - 1 - dim))
    return level


def normal_values(stream_key, shape, scale, most, pieces=(), kind=jnp.bfloat16):
    array = jax.random.normal(stream_key, shape, jnp.float32) * scale
    if len(pieces) > 0:
        array = shard_levels(stream_key, shape, pieces, -0.22, 0.18) * array
    return jnp.clip(array, min=-most, max=most).astype(kind)


def setup_inputs(seed: int = 0) -> dict:
    streams_of = jax.random.split(jax.random.key(seed), 5)
    return {
        "density": jnp.clip(jnp.exp(math.log(2.0) - 1.3862944 * jax.random.uniform(streams_of[0], (Z, NR, NPHI), jnp.float32) ** shard_levels(streams_of[0], (Z, NR, NPHI), ((1, 4), (2, 32)), -0.2, 0.2)), 0.5, 2.0),
        "carried": normal_values(streams_of[1], (7, Z, NR, NPHI), 0.3, 1.5, ((2, 4), (3, 32)), jnp.float32),
        "cycle_shift": plant(jax.random.randint(streams_of[2], (NR,), 0, NPHI), jax.random.fold_in(streams_of[2], 1), 0, NPHI - 1).astype(jnp.int32),
        "cycle_fraction": jnp.clip(1.0 * jax.random.uniform(streams_of[3], (NR,), jnp.float32) ** shard_levels(streams_of[3], (NR,), ((0, 4),), -0.2, 0.2), 0.0, 1.0),
    }


def face_divergence(padded, axis, direction):
    count = padded.shape[axis] - 2
    left = jax.lax.slice_in_dim(padded, 0, count + 1, axis=axis)
    right = jax.lax.slice_in_dim(padded, 1, count + 2, axis=axis)
    q_left = left[:8]
    q_right = right[:8]
    v_left = left[8 + direction][None]
    v_right = right[8 + direction][None]
    speed = jnp.maximum(jnp.abs(v_left), jnp.abs(v_right)) + 1.0
    flux = 0.5 * (v_left * q_left + v_right * q_right) - 0.5 * speed * (q_right - q_left)
    upper = jax.lax.slice_in_dim(flux, 1, count + 1, axis=axis)
    lower = jax.lax.slice_in_dim(flux, 0, count, axis=axis)
    return upper - lower


def reference(density, carried, cycle_shift, cycle_fraction):
    state = jnp.concatenate([density[None], carried], axis=0)
    velocity = carried[0:3] / density[None]
    extended = jnp.concatenate([state, velocity], axis=0)
    zeros_cycle = jnp.zeros_like(extended[:, :, :1, :])
    radial = jnp.concatenate([zeros_cycle, extended, zeros_cycle], axis=2)
    azimuth = jnp.concatenate([extended[:, :, :, -1:], extended, extended[:, :, :, :1]], axis=3)
    height = jnp.concatenate([extended[:, -1:], extended, extended[:, :1]], axis=1)
    update = 0.08 * (face_divergence(radial, 2, 0) + face_divergence(azimuth, 3, 1) + face_divergence(height, 1, 2))
    cells = jnp.arange(NPHI, dtype=jnp.int32)
    first = (cells[None, :] - cycle_shift[:, None]) % NPHI
    second = (cells[None, :] - cycle_shift[:, None] - 1) % NPHI
    first = jnp.broadcast_to(first[None, None], state.shape).astype(jnp.int32)
    second = jnp.broadcast_to(second[None, None], state.shape).astype(jnp.int32)
    part_one = jnp.take_along_axis(state, first, axis=3)
    part_two = jnp.take_along_axis(state, second, axis=3)
    weight = cycle_fraction[None, None, :, None]
    new_state = (1.0 - weight) * part_one + weight * part_two - update
    return new_state[0], new_state[1:]
```

```python
import functools

import jax
import jax.numpy as jnp
from jax import lax
from jax.experimental import pallas as pl
from jax.experimental.pallas import tpu as pltpu
from jax.sharding import PartitionSpec as P

FIELDS = 8
ROWS = 8
LANES = 128


def neighbours(value, axis, step, wrap):
    count = lax.axis_size(axis)
    pairs = [(i, i + step) for i in range(count)]
    if wrap:
        pairs = [(i, j % count) for i, j in pairs]
    else:
        pairs = [(i, j) for i, j in pairs if 0 <= j < count]
    return lax.ppermute(value, axis, pairs)


def shift_kernel(blocks, tiles, shift_ref, fraction_ref, x_ref, o_ref):
    total = blocks * tiles
    lane = lax.broadcasted_iota(jnp.int32, (FIELDS, LANES), 1)
    shifts = [shift_ref[row] for row in range(ROWS)]
    whole = [s // LANES for s in shifts]
    part = [s % LANES for s in shifts]
    fraction = [fraction_ref[row] for row in range(ROWS)]

    def place(row, tile):
        start = (tile // tiles) * (FIELDS * tiles * ROWS) + (tile % tiles) * ROWS + row
        return pl.ds(start, FIELDS, stride=tiles * ROWS)

    def turned(row, tile):
        tile = lax.rem(tile - whole[row] + 2 * total, total)
        return pltpu.roll(x_ref[place(row, tile), :], part[row], 1)

    def step(tile, row, carry):
        turned_before, moved_before = carry
        now = turned(row, tile)
        first = jnp.where(lane >= part[row], now, turned_before)
        rolled = pltpu.roll(first, 1, 1)
        second = jnp.where(lane >= 1, rolled, moved_before)
        value = (1.0 - fraction[row]) * first + fraction[row] * second
        return value, (now, rolled)

    carries = []
    for row in range(ROWS):
        before = turned(row, -2)
        _, carry = step(-1, row, (before, before))
        carries.append(carry)

    def body(block, carries):
        carries = list(carries)
        for t in range(tiles):
            for row in range(ROWS):
                value, carries[row] = step(block * tiles + t, row, carries[row])
                o_ref[place(row, block * tiles + t), :] = value
        return tuple(carries)

    lax.fori_loop(0, blocks, body, tuple(carries))


def shift_rows(received, shifts, fractions, blocks, tiles):
    flat = received.reshape(-1, LANES)
    out = pl.pallas_call(
        functools.partial(shift_kernel, blocks, tiles),
        out_shape=jax.ShapeDtypeStruct(flat.shape, flat.dtype),
        in_specs=[
            pl.BlockSpec(memory_space=pltpu.SMEM),
            pl.BlockSpec(memory_space=pltpu.SMEM),
            pl.BlockSpec(memory_space=pltpu.VMEM),
        ],
        out_specs=pl.BlockSpec(memory_space=pltpu.VMEM),
        cost_estimate=pl.CostEstimate(
            flops=8 * flat.size, bytes_accessed=8 * flat.size, transcendentals=0
        ),
        compiler_params=pltpu.CompilerParams(vmem_limit_bytes=24 * 2**20),
        name="shift_rows",
    )(shifts, fractions, flat)
    return out.reshape(received.shape)


def flux2(v_left, v_right, speed, q_left, q_right):
    return v_left * q_left + v_right * q_right - speed * (q_right - q_left)


def face_speed(v_left, v_right):
    return jnp.maximum(jnp.abs(v_left), jnp.abs(v_right)) + 1.0


def update_kernel(
    groups, width, density_ref, carried_ref, inner_ref, outer_ref, left_ref, right_ref, o_ref, lower_ref
):
    column = lax.broadcasted_iota(jnp.int32, (ROWS, width), 1)
    sub = lax.broadcasted_iota(jnp.int32, (ROWS, width), 0)

    def field(c, z, rows):
        return density_ref[z, rows, :] if c == 0 else carried_ref[c - 1, z, rows, :]

    def edge(ref, c, z):
        return jnp.broadcast_to(ref[c, z], (ROWS, width))

    def edge_velocity(ref, z):
        rho = edge(ref, 0, z)
        return edge(ref, 1, z) / jnp.where(rho == 0.0, 1.0, rho)

    for z in range(2):
        v_left = edge_velocity(inner_ref, z)
        v_right = field(1, z, pl.ds(0, ROWS)) / field(0, z, pl.ds(0, ROWS))
        v_right = jnp.broadcast_to(v_right[0:1], (ROWS, width))
        speed = face_speed(v_left, v_right)
        for c in range(FIELDS):
            q_right = jnp.broadcast_to(field(c, z, pl.ds(0, ROWS))[0:1], (ROWS, width))
            lower_ref[c, z] = flux2(v_left, v_right, speed, edge(inner_ref, c, z), q_right)

    def body(g, _):
        rows = pl.ds(pl.multiple_of(g * ROWS, ROWS), ROWS)
        after = pl.ds(pl.multiple_of(jnp.minimum(g + 1, groups - 1) * ROWS, ROWS), ROWS)
        last = g == groups - 1
        left, right = left_ref[rows, :], right_ref[rows, :]

        def at(block, c, z):
            return block[:, 2 * c + z : 2 * c + z + 1]

        rho = [field(0, z, rows) for z in range(2)]
        v_height = [field(3, z, rows) / rho[z] for z in range(2)]
        speed_height = 2.0 * face_speed(v_height[0], v_height[1])
        for z in range(2):
            other = 1 - z
            v_r = field(1, z, rows) / rho[z]
            v_a = field(2, z, rows) / rho[z]
            v_r_next = jnp.where(
                last, edge_velocity(outer_ref, z), field(1, z, after) / field(0, z, after)
            )
            v_r_up = pltpu.roll(jnp.where(sub == 0, v_r_next, v_r), ROWS - 1, 0)
            speed_r = face_speed(v_r, v_r_up)
            v_a_left = at(left, 2, z) / at(left, 0, z)
            v_a_right = at(right, 2, z) / at(right, 0, z)
            v_a_up = jnp.where(column == width - 1, v_a_right, pltpu.roll(v_a, width - 1, 1))
            speed_a = face_speed(v_a, v_a_up)
            speed_left = face_speed(v_a_left, v_a[:, 0:1])
            for c in range(FIELDS):
                q = field(c, z, rows)
                q_next = jnp.where(last, edge(outer_ref, c, z), field(c, z, after))
                q_up = pltpu.roll(jnp.where(sub == 0, q_next, q), ROWS - 1, 0)
                upper = flux2(v_r, v_r_up, speed_r, q, q_up)
                lower = pltpu.roll(jnp.where(sub == ROWS - 1, lower_ref[c, z], upper), 1, 0)
                lower_ref[c, z] = upper
                total = upper - lower
                q_up = jnp.where(column == width - 1, at(right, c, z), pltpu.roll(q, width - 1, 1))
                upper = flux2(v_a, v_a_up, speed_a, q, q_up)
                first = flux2(v_a_left, v_a[:, 0:1], speed_left, at(left, c, z), q[:, 0:1])
                lower = jnp.where(column == 0, first, pltpu.roll(upper, 1, 1))
                total = total + (upper - lower)
                total = total + speed_height * (q - field(c, other, rows))
                o_ref[c, z, rows, :] = 0.04 * total
        return 0

    lax.fori_loop(0, groups, body, 0)


def update_of(density, carried, inner, outer, left, right):
    rows, width = density.shape[1:]
    size = FIELDS * density.size
    vmem = pl.BlockSpec(memory_space=pltpu.VMEM)
    return pl.pallas_call(
        functools.partial(update_kernel, rows // ROWS, width),
        out_shape=jax.ShapeDtypeStruct((FIELDS,) + density.shape, density.dtype),
        in_specs=[vmem] * 6,
        out_specs=vmem,
        scratch_shapes=[pltpu.VMEM((FIELDS, 2, ROWS, width), jnp.float32)],
        cost_estimate=pl.CostEstimate(flops=40 * size, bytes_accessed=8 * size, transcendentals=0),
        compiler_params=pltpu.CompilerParams(vmem_limit_bytes=24 * 2**20),
        name="flux_update",
    )(density, carried, inner, outer, left, right)


def local(density, carried, cycle_shift, cycle_fraction):
    height, rows, width = density.shape
    devices = lax.axis_size("phi")
    groups, tiles = rows // ROWS, width // LANES
    state = jnp.concatenate([density[None], carried], axis=0)
    sent = state.reshape(FIELDS, height, groups, ROWS, tiles, LANES)
    sent = sent.transpose(2, 1, 0, 4, 3, 5).reshape(devices, FIELDS, tiles, ROWS, LANES)
    received = lax.all_to_all(sent, "phi", 0, 0, tiled=True)

    inner = neighbours(state[:, :, -1:], "rad", 1, False)
    outer = neighbours(state[:, :, :1], "rad", -1, False)
    left = neighbours(state[:, :, :, -1], "phi", 1, True)
    right = neighbours(state[:, :, :, 0], "phi", -1, True)
    left = left.reshape(FIELDS * height, rows).T
    right = right.reshape(FIELDS * height, rows).T
    update = update_of(density, carried, inner, outer, left, right)

    group = lax.axis_index("phi") // height
    shifts = lax.dynamic_slice_in_dim(cycle_shift, group * ROWS, ROWS)
    fractions = lax.dynamic_slice_in_dim(cycle_fraction, group * ROWS, ROWS)
    moved = shift_rows(received, shifts, fractions, devices, tiles)
    moved = lax.all_to_all(moved, "phi", 0, 0, tiled=True)
    moved = moved.reshape(groups, height, FIELDS, tiles, ROWS, LANES).transpose(2, 1, 0, 4, 3, 5)
    new_state = moved.reshape(state.shape) - update
    return new_state[0], new_state[1:]


def solution(mesh):
    placed = (P(None, "rad", "phi"), P(None, None, "rad", "phi"), P("rad"), P("rad"))
    return jax.shard_map(
        local,
        mesh=mesh,
        in_specs=placed,
        out_specs=(P(None, "rad", "phi"), P(None, None, "rad", "phi")),
        check_vma=False,
    )
```

```python
import functools

import jax
import jax.numpy as jnp
from jax import lax
from jax.experimental import pallas as pl
from jax.experimental.pallas import tpu as pltpu
from jax.sharding import PartitionSpec as P

FIELDS = 8
ROWS = 8
LANES = 128


def neighbours(value, axis, step, wrap):
    count = lax.axis_size(axis)
    pairs = [(i, i + step) for i in range(count)]
    if wrap:
        pairs = [(i, j % count) for i, j in pairs]
    else:
        pairs = [(i, j) for i, j in pairs if 0 <= j < count]
    return lax.ppermute(value, axis, pairs)


def in_hbm(value):
    return pltpu.with_memory_space_constraint(value, pltpu.HBM)


def pack_kernel(groups, height, chunks, density_ref, carried_ref, o_ref, taken, packed, in_sems, out_sems):
    size = groups // chunks
    arrivals, departures = [], []
    for i in range(chunks):
        piece = pl.ds(i * size, size)
        ends = ((density_ref.at[:, piece], taken.at[0, :, piece]), (carried_ref.at[:, :, piece], taken.at[1:, :, piece]))
        arrivals.append([pltpu.make_async_copy(*pair, in_sems.at[i, k]) for k, pair in enumerate(ends)])
        for copy in arrivals[i]:
            copy.start()
    for i in range(chunks):
        piece = pl.ds(i * size, size)
        for copy in arrivals[i]:
            copy.wait()

        def reorder(g, _):
            for z in range(height):
                for c in range(FIELDS):
                    packed[g, z, c] = taken[c, z, g]
            return 0

        lax.fori_loop(i * size, (i + 1) * size, reorder, 0)
        departures.append(pltpu.make_async_copy(packed.at[piece], o_ref.at[piece], out_sems.at[i]))
        departures[i].start()
    for copy in departures:
        copy.wait()


def pack(density, carried, chunks=8):
    height, rows, width = density.shape
    groups = rows // ROWS
    natural = (height, groups, ROWS, width)
    shape = (groups, height, FIELDS, ROWS, width)
    hbm = pl.BlockSpec(memory_space=pltpu.HBM)
    return pl.pallas_call(
        functools.partial(pack_kernel, groups, height, chunks),
        out_shape=pltpu.HBM(shape, density.dtype),
        in_specs=[hbm, hbm],
        out_specs=hbm,
        scratch_shapes=[
            pltpu.VMEM((FIELDS,) + natural, jnp.float32),
            pltpu.VMEM(shape, jnp.float32),
            pltpu.SemaphoreType.DMA((chunks, 2)),
            pltpu.SemaphoreType.DMA((chunks,)),
        ],
        cost_estimate=pl.CostEstimate(flops=0, bytes_accessed=64 * density.size, transcendentals=0),
        compiler_params=pltpu.CompilerParams(vmem_limit_bytes=12 * 2**20),
        name="pack",
    )(in_hbm(density.reshape(natural)), in_hbm(carried.reshape((FIELDS - 1,) + natural)))


def exchanged(registers, sub):
    values = list(registers)
    for k in (4, 2, 1):
        low = (sub & k) == 0
        result = list(values)
        for i in range(ROWS):
            if not i & k:
                a, b = values[i], values[i + k]
                result[i] = jnp.where(low, a, pltpu.roll(b, k, 0))
                result[i + k] = jnp.where(low, pltpu.roll(a, ROWS - k, 0), b)
        values = result
    return values


def shift_kernel(
    blocks, tiles, chunks, shift_ref, fraction_ref, x_ref, o_ref, taken, cycles, placed, in_sems, out_sems
):
    size = blocks // chunks
    total = blocks * tiles
    lane = lax.broadcasted_iota(jnp.int32, (FIELDS, LANES), 1)
    sub = lax.broadcasted_iota(jnp.int32, (FIELDS, LANES), 0)
    shifts = [shift_ref[row] for row in range(ROWS)]
    whole = [s // LANES for s in shifts]
    part = [s % LANES for s in shifts]
    fraction = [fraction_ref[row] for row in range(ROWS)]

    def lanes(t):
        return pl.ds(t * LANES, LANES)

    arrivals = []
    for i in range(chunks):
        piece = pl.ds(i * size, size)
        arrivals.append(pltpu.make_async_copy(x_ref.at[piece], taken.at[piece], in_sems.at[i]))
        arrivals[i].start()

    def collect(block, _):
        for t in range(tiles):
            by_row = exchanged([taken[block, c, :, lanes(t)] for c in range(FIELDS)], sub)
            for row in range(ROWS):
                cycles[row, block * tiles + t] = by_row[row]
        return 0

    for i in range(chunks):
        arrivals[i].wait()
        lax.fori_loop(i * size, (i + 1) * size, collect, 0, unroll=4)

    def turned(row, tile):
        return pltpu.roll(cycles[row, (tile - whole[row]) & (total - 1)], part[row], 1)

    def step(tile, row, carry):
        turned_before, moved_before = carry
        now = turned(row, tile)
        first = jnp.where(lane >= part[row], now, turned_before)
        rolled = pltpu.roll(first, 1, 1)
        second = jnp.where(lane >= 1, rolled, moved_before)
        value = (1.0 - fraction[row]) * first + fraction[row] * second
        return value, (now, rolled)

    def place(block, carries):
        carries = list(carries)
        for t in range(tiles):
            by_row = []
            for row in range(ROWS):
                value, carries[row] = step(block * tiles + t, row, carries[row])
                by_row.append(value)
            by_field = exchanged(by_row, sub)
            for c in range(FIELDS):
                placed[block, c, :, lanes(t)] = by_field[c]
        return tuple(carries)

    carries = []
    for row in range(ROWS):
        before = turned(row, -2)
        carries.append(step(-1, row, (before, before))[1])
    carries = tuple(carries)
    departures = []
    for i in range(chunks):
        piece = pl.ds(i * size, size)
        carries = lax.fori_loop(i * size, (i + 1) * size, place, carries, unroll=4)
        departures.append(pltpu.make_async_copy(placed.at[piece], o_ref.at[piece], out_sems.at[i]))
        departures[i].start()
    for copy in departures:
        copy.wait()


def shift_rows(received, shifts, fractions, chunks=8):
    blocks, _, _, width = received.shape
    tiles = width // LANES
    smem, hbm = pl.BlockSpec(memory_space=pltpu.SMEM), pl.BlockSpec(memory_space=pltpu.HBM)
    return pl.pallas_call(
        functools.partial(shift_kernel, blocks, tiles, chunks),
        out_shape=pltpu.HBM(received.shape, received.dtype),
        in_specs=[smem, smem, hbm],
        out_specs=hbm,
        scratch_shapes=[
            pltpu.VMEM(received.shape, jnp.float32),
            pltpu.VMEM((ROWS, blocks * tiles, FIELDS, LANES), jnp.float32),
            pltpu.VMEM(received.shape, jnp.float32),
            pltpu.SemaphoreType.DMA((chunks,)),
            pltpu.SemaphoreType.DMA((chunks,)),
        ],
        cost_estimate=pl.CostEstimate(
            flops=8 * received.size, bytes_accessed=8 * received.size, transcendentals=0
        ),
        compiler_params=pltpu.CompilerParams(vmem_limit_bytes=20 * 2**20),
        name="shift_rows",
    )(shifts, fractions, in_hbm(received))


def finish_kernel(groups, height, chunks, moved_ref, update_ref, density_ref, carried_ref, taken, change, new, in_sems, out_sems):
    size = groups // chunks
    arrivals, departures = [], []
    for i in range(chunks):
        piece = pl.ds(i * size, size)
        arrivals.append(
            (
                pltpu.make_async_copy(moved_ref.at[piece], taken.at[piece], in_sems.at[i, 0]),
                pltpu.make_async_copy(update_ref.at[:, :, piece], change.at[:, :, piece], in_sems.at[i, 1]),
            )
        )
        for copy in arrivals[i]:
            copy.start()
    for i in range(chunks):
        piece = pl.ds(i * size, size)
        for copy in arrivals[i]:
            copy.wait()

        def subtract(g, _):
            for z in range(height):
                for c in range(FIELDS):
                    new[c, z, g] = taken[g, z, c] - change[c, z, g]
            return 0

        lax.fori_loop(i * size, (i + 1) * size, subtract, 0)
        ends = ((new.at[0, :, piece], density_ref.at[:, piece]), (new.at[1:, :, piece], carried_ref.at[:, :, piece]))
        for k, (source, target) in enumerate(ends):
            departures.append(pltpu.make_async_copy(source, target, out_sems.at[i, k]))
            departures[-1].start()
    for copy in departures:
        copy.wait()


def finish(moved, update, chunks=8):
    groups, height, _, _, width = moved.shape
    hbm = pl.BlockSpec(memory_space=pltpu.HBM)
    natural = (height, groups, ROWS, width)
    return pl.pallas_call(
        functools.partial(finish_kernel, groups, height, chunks),
        out_shape=[
            jax.ShapeDtypeStruct(natural, jnp.float32),
            jax.ShapeDtypeStruct((FIELDS - 1,) + natural, jnp.float32),
        ],
        in_specs=[hbm, hbm],
        out_specs=[hbm, hbm],
        scratch_shapes=[
            pltpu.VMEM(moved.shape, jnp.float32),
            pltpu.VMEM((FIELDS,) + natural, jnp.float32),
            pltpu.VMEM((FIELDS,) + natural, jnp.float32),
            pltpu.SemaphoreType.DMA((chunks, 2)),
            pltpu.SemaphoreType.DMA((chunks, 2)),
        ],
        cost_estimate=pl.CostEstimate(flops=moved.size, bytes_accessed=12 * moved.size, transcendentals=0),
        compiler_params=pltpu.CompilerParams(vmem_limit_bytes=20 * 2**20),
        name="finish",
    )(in_hbm(moved), in_hbm(update.reshape((FIELDS,) + natural)))


def flux2(v_left, v_right, speed, q_left, q_right):
    return v_left * q_left + v_right * q_right - speed * (q_right - q_left)


def face_speed(v_left, v_right):
    return jnp.maximum(jnp.abs(v_left), jnp.abs(v_right)) + 1.0


def update_kernel(
    groups, width, density_ref, carried_ref, inner_ref, outer_ref, left_ref, right_ref, o_ref, lower_ref
):
    column = lax.broadcasted_iota(jnp.int32, (ROWS, width), 1)
    sub = lax.broadcasted_iota(jnp.int32, (ROWS, width), 0)

    def field(c, z, rows):
        return density_ref[z, rows, :] if c == 0 else carried_ref[c - 1, z, rows, :]

    def edge(ref, c, z):
        return jnp.broadcast_to(ref[c, z], (ROWS, width))

    def edge_velocity(ref, z):
        rho = edge(ref, 0, z)
        return edge(ref, 1, z) / jnp.where(rho == 0.0, 1.0, rho)

    for z in range(2):
        v_left = edge_velocity(inner_ref, z)
        v_right = field(1, z, pl.ds(0, ROWS)) / field(0, z, pl.ds(0, ROWS))
        v_right = jnp.broadcast_to(v_right[0:1], (ROWS, width))
        speed = face_speed(v_left, v_right)
        for c in range(FIELDS):
            q_right = jnp.broadcast_to(field(c, z, pl.ds(0, ROWS))[0:1], (ROWS, width))
            lower_ref[c, z] = flux2(v_left, v_right, speed, edge(inner_ref, c, z), q_right)

    def body(g, _):
        rows = pl.ds(pl.multiple_of(g * ROWS, ROWS), ROWS)
        after = pl.ds(pl.multiple_of(jnp.minimum(g + 1, groups - 1) * ROWS, ROWS), ROWS)
        last = g == groups - 1
        left, right = left_ref[rows, :], right_ref[rows, :]

        def at(block, c, z):
            return block[:, 2 * c + z : 2 * c + z + 1]

        rho = [field(0, z, rows) for z in range(2)]
        v_height = [field(3, z, rows) / rho[z] for z in range(2)]
        speed_height = 2.0 * face_speed(v_height[0], v_height[1])
        for z in range(2):
            other = 1 - z
            v_r = field(1, z, rows) / rho[z]
            v_a = field(2, z, rows) / rho[z]
            v_r_next = jnp.where(
                last, edge_velocity(outer_ref, z), field(1, z, after) / field(0, z, after)
            )
            v_r_up = pltpu.roll(jnp.where(sub == 0, v_r_next, v_r), ROWS - 1, 0)
            speed_r = face_speed(v_r, v_r_up)
            v_a_left = at(left, 2, z) / at(left, 0, z)
            v_a_right = at(right, 2, z) / at(right, 0, z)
            v_a_up = jnp.where(column == width - 1, v_a_right, pltpu.roll(v_a, width - 1, 1))
            speed_a = face_speed(v_a, v_a_up)
            speed_left = face_speed(v_a_left, v_a[:, 0:1])
            for c in range(FIELDS):
                q = field(c, z, rows)
                q_next = jnp.where(last, edge(outer_ref, c, z), field(c, z, after))
                q_up = pltpu.roll(jnp.where(sub == 0, q_next, q), ROWS - 1, 0)
                upper = flux2(v_r, v_r_up, speed_r, q, q_up)
                lower = pltpu.roll(jnp.where(sub == ROWS - 1, lower_ref[c, z], upper), 1, 0)
                lower_ref[c, z] = upper
                total = upper - lower
                q_up = jnp.where(column == width - 1, at(right, c, z), pltpu.roll(q, width - 1, 1))
                upper = flux2(v_a, v_a_up, speed_a, q, q_up)
                first = flux2(v_a_left, v_a[:, 0:1], speed_left, at(left, c, z), q[:, 0:1])
                lower = jnp.where(column == 0, first, pltpu.roll(upper, 1, 1))
                total = total + (upper - lower)
                total = total + speed_height * (q - field(c, other, rows))
                o_ref[c, z, rows, :] = 0.04 * total
        return 0

    lax.fori_loop(0, groups, body, 0)


def update_of(density, carried, inner, outer, left, right):
    rows, width = density.shape[1:]
    size = FIELDS * density.size
    vmem = pl.BlockSpec(memory_space=pltpu.VMEM)
    return pl.pallas_call(
        functools.partial(update_kernel, rows // ROWS, width),
        out_shape=pltpu.HBM((FIELDS,) + density.shape, density.dtype),
        in_specs=[vmem] * 6,
        out_specs=vmem,
        scratch_shapes=[pltpu.VMEM((FIELDS, 2, ROWS, width), jnp.float32)],
        cost_estimate=pl.CostEstimate(flops=40 * size, bytes_accessed=8 * size, transcendentals=0),
        compiler_params=pltpu.CompilerParams(vmem_limit_bytes=24 * 2**20),
        name="flux_update",
    )(density, carried, inner, outer, left, right)


def local(density, carried, cycle_shift, cycle_fraction):
    height, rows, width = density.shape
    devices = lax.axis_size("phi")
    packed = pack(density, carried)
    received = lax.all_to_all(
        packed.reshape(devices, FIELDS, ROWS, width), "phi", 0, 0, tiled=True
    )

    state = jnp.concatenate([density[None], carried], axis=0)
    inner = neighbours(state[:, :, -1:], "rad", 1, False)
    outer = neighbours(state[:, :, :1], "rad", -1, False)
    left = neighbours(state[:, :, :, -1], "phi", 1, True)
    right = neighbours(state[:, :, :, 0], "phi", -1, True)
    left = left.reshape(FIELDS * height, rows).T
    right = right.reshape(FIELDS * height, rows).T

    group = lax.axis_index("phi") // height
    shifts = lax.dynamic_slice_in_dim(cycle_shift, group * ROWS, ROWS)
    fractions = lax.dynamic_slice_in_dim(cycle_fraction, group * ROWS, ROWS)
    received, inner, outer, left, right = lax.optimization_barrier(
        (received, inner, outer, left, right)
    )
    moved = shift_rows(received, shifts, fractions)
    moved, inner, outer, left, right = lax.optimization_barrier(
        (moved, inner, outer, left, right)
    )
    moved = lax.all_to_all(moved, "phi", 0, 0, tiled=True)
    update = update_of(density, carried, inner, outer, left, right)
    density_next, carried_next = finish(moved.reshape(packed.shape), update)
    return density_next.reshape(density.shape), carried_next.reshape(carried.shape)


def solution(mesh):
    placed = (P(None, "rad", "phi"), P(None, None, "rad", "phi"), P("rad"), P("rad"))
    return jax.shard_map(
        local,
        mesh=mesh,
        in_specs=placed,
        out_specs=(P(None, "rad", "phi"), P(None, None, "rad", "phi")),
        check_vma=False,
    )
```

```python
import functools

import jax
import jax.numpy as jnp
from jax import lax
from jax.experimental import pallas as pl
from jax.experimental.pallas import tpu as pltpu
from jax.sharding import PartitionSpec as P

FIELDS = 8
ROWS = 8
LANES = 128


def neighbours(value, axis, step, wrap):
    count = lax.axis_size(axis)
    pairs = [(i, i + step) for i in range(count)]
    if wrap:
        pairs = [(i, j % count) for i, j in pairs]
    else:
        pairs = [(i, j) for i, j in pairs if 0 <= j < count]
    return lax.ppermute(value, axis, pairs)


def in_hbm(value):
    return pltpu.with_memory_space_constraint(value, pltpu.HBM)


def pack_kernel(height, density_ref, carried_ref, o_ref, sems):
    copies = []
    for c in range(FIELDS):
        for z in range(height):
            source = density_ref.at[z] if c == 0 else carried_ref.at[c - 1, z]
            copies.append(pltpu.make_async_copy(source, o_ref.at[:, z, c], sems.at[c, z]))
    for copy in copies:
        copy.start()
    for copy in copies:
        copy.wait()


def pack(density, carried):
    height, rows, width = density.shape
    groups = rows // ROWS
    natural = (height, groups, ROWS, width)
    hbm = pl.BlockSpec(memory_space=pltpu.HBM)
    return pl.pallas_call(
        functools.partial(pack_kernel, height),
        out_shape=pltpu.VMEM((groups, height, FIELDS, ROWS, width), density.dtype),
        in_specs=[hbm, hbm],
        out_specs=pl.BlockSpec(memory_space=pltpu.VMEM),
        scratch_shapes=[pltpu.SemaphoreType.DMA((FIELDS, height))],
        cost_estimate=pl.CostEstimate(flops=0, bytes_accessed=64 * density.size, transcendentals=0),
        compiler_params=pltpu.CompilerParams(vmem_limit_bytes=8 * 2**20),
        name="pack",
    )(in_hbm(density.reshape(natural)), in_hbm(carried.reshape((FIELDS - 1,) + natural)))


def exchanged(registers, sub):
    values = list(registers)
    for k in (4, 2, 1):
        low = (sub & k) == 0
        result = list(values)
        for i in range(ROWS):
            if not i & k:
                a, b = values[i], values[i + k]
                result[i] = jnp.where(low, a, pltpu.roll(b, k, 0))
                result[i + k] = jnp.where(low, pltpu.roll(a, ROWS - k, 0), b)
        values = result
    return values


def shift_kernel(
    blocks, tiles, chunks, height, shift_ref, fraction_ref, x_ref, o_ref, cycles, placed, out_sems
):
    size = blocks // chunks
    total = blocks * tiles
    lane = lax.broadcasted_iota(jnp.int32, (FIELDS, LANES), 1)
    sub = lax.broadcasted_iota(jnp.int32, (FIELDS, LANES), 0)
    base = (lax.axis_index("phi") // height) * ROWS
    shifts = [shift_ref[base + row] for row in range(ROWS)]
    whole = [s // LANES for s in shifts]
    part = [s % LANES for s in shifts]
    fraction = [fraction_ref[base + row] for row in range(ROWS)]

    def lanes(t):
        return pl.ds(t * LANES, LANES)

    def collect(block, _):
        for t in range(tiles):
            by_row = exchanged([x_ref[block, c, :, lanes(t)] for c in range(FIELDS)], sub)
            for row in range(ROWS):
                cycles[row, block * tiles + t] = by_row[row]
        return 0

    lax.fori_loop(0, blocks, collect, 0, unroll=4)

    def turned(row, tile):
        return pltpu.roll(cycles[row, (tile - whole[row]) & (total - 1)], part[row], 1)

    def step(tile, row, carry):
        turned_before, moved_before = carry
        now = turned(row, tile)
        first = jnp.where(lane >= part[row], now, turned_before)
        rolled = pltpu.roll(first, 1, 1)
        second = jnp.where(lane >= 1, rolled, moved_before)
        value = (1.0 - fraction[row]) * first + fraction[row] * second
        return value, (now, rolled)

    def place(block, carries):
        carries = list(carries)
        for t in range(tiles):
            by_row = []
            for row in range(ROWS):
                value, carries[row] = step(block * tiles + t, row, carries[row])
                by_row.append(value)
            by_field = exchanged(by_row, sub)
            for c in range(FIELDS):
                placed[block, c, :, lanes(t)] = by_field[c]
        return tuple(carries)

    carries = []
    for row in range(ROWS):
        before = turned(row, -2)
        carries.append(step(-1, row, (before, before))[1])
    carries = tuple(carries)
    departures = []
    for i in range(chunks):
        piece = pl.ds(i * size, size)
        carries = lax.fori_loop(i * size, (i + 1) * size, place, carries, unroll=4)
        departures.append(pltpu.make_async_copy(placed.at[piece], o_ref.at[piece], out_sems.at[i]))
        departures[i].start()
    for copy in departures:
        copy.wait()


def shift_rows(received, shifts, fractions, height, chunks=8):
    blocks, _, _, width = received.shape
    tiles = width // LANES
    smem, hbm = pl.BlockSpec(memory_space=pltpu.SMEM), pl.BlockSpec(memory_space=pltpu.HBM)
    return pl.pallas_call(
        functools.partial(shift_kernel, blocks, tiles, chunks, height),
        out_shape=pltpu.HBM(received.shape, received.dtype),
        in_specs=[smem, smem, pl.BlockSpec(memory_space=pltpu.VMEM)],
        out_specs=hbm,
        scratch_shapes=[
            pltpu.VMEM((ROWS, blocks * tiles, FIELDS, LANES), jnp.float32),
            pltpu.VMEM(received.shape, jnp.float32),
            pltpu.SemaphoreType.DMA((chunks,)),
        ],
        cost_estimate=pl.CostEstimate(
            flops=8 * received.size, bytes_accessed=8 * received.size, transcendentals=0
        ),
        compiler_params=pltpu.CompilerParams(vmem_limit_bytes=20 * 2**20),
        name="shift_rows",
    )(shifts, fractions, pltpu.with_memory_space_constraint(received, pltpu.VMEM))


def edge_fluxes(height, inner, first_rows, last_rows, outer, left, first_cells, last_cells, right, rows_ref, cells_ref):
    def layer(ref, c):
        return ref[c * height : (c + 1) * height, :]

    def radial(ref):
        rho = layer(ref, 0)
        return layer(ref, 1) / jnp.where(rho == 0.0, 1.0, rho)

    for lower, upper, sign, start in ((inner, first_rows, 0.04, 0), (last_rows, outer, -0.04, FIELDS * height)):
        v_lower, v_upper = radial(lower), radial(upper)
        speed = face_speed(v_lower, v_upper)
        for c in range(FIELDS):
            flux = flux2(v_lower, v_upper, speed, layer(lower, c), layer(upper, c))
            rows_ref[start + c * height : start + (c + 1) * height, :] = sign * flux

    odd = lax.broadcasted_iota(jnp.int32, cells_ref.shape, 1) % 2 == 1

    def azimuthal(cells):
        v = [cells[:, 4 + z : 5 + z] / cells[:, z : z + 1] for z in range(2)]
        return jnp.where(odd, v[1], v[0])

    def flux(lower, upper):
        v_lower, v_upper = azimuthal(lower), azimuthal(upper)
        return 0.04 * flux2(v_lower, v_upper, face_speed(v_lower, v_upper), lower, upper)

    upper_faces = pltpu.roll(flux(last_cells[...], right[...]), FIELDS * height, 1)
    cells_ref[...] = flux(left[...], first_cells[...]) - upper_faces


def finish_kernel(
    groups,
    height,
    chunks,
    moved_ref,
    update_ref,
    *refs,
):
    row_refs, cell_refs = refs[:4], refs[4:8]
    density_ref, carried_ref, layer_rows, layer_cells, taken, change, edge_rows, edge_cells, new = refs[8:17]
    edge_sems, in_sems, out_sems = refs[17:]
    size = groups // chunks
    width = moved_ref.shape[-1]
    lane = lax.broadcasted_iota(jnp.int32, (ROWS, LANES), 1)
    edges = []
    for i in range(4):
        edges.append(pltpu.make_async_copy(row_refs[i], layer_rows.at[i], edge_sems.at[0, i]))
        edges.append(pltpu.make_async_copy(cell_refs[i], layer_cells.at[i], edge_sems.at[1, i]))
    for copy in edges:
        copy.start()
    arrivals, departures = [], []
    for i in range(chunks):
        piece = pl.ds(i * size, size)
        ends = ((moved_ref.at[piece], taken.at[piece]), (update_ref.at[:, :, piece], change.at[:, :, piece]))
        arrivals.append([pltpu.make_async_copy(*pair, in_sems.at[i, k]) for k, pair in enumerate(ends)])
        for copy in arrivals[i]:
            copy.start()
    for copy in edges:
        copy.wait()
    layers = [layer_rows.at[i] for i in range(4)] + [layer_cells.at[i] for i in range(4)]
    edge_fluxes(height, *layers, edge_rows, edge_cells)

    def subtract(g, _):
        cells = edge_cells[pl.ds(pl.multiple_of(g * ROWS, ROWS), ROWS), :]
        for z in range(height):
            for c in range(FIELDS):
                k = c * height + z
                for at in range(0, width, LANES):
                    value = taken[g, z, c, :, at : at + LANES] - change[c, z, g, :, at : at + LANES]
                    if at == 0:
                        value = value + jnp.where(lane == 0, cells[:, k : k + 1], 0.0)
                    if at == width - LANES:
                        m = FIELDS * height + k
                        value = value + jnp.where(lane == LANES - 1, cells[:, m : m + 1], 0.0)
                    new[c, z, g, :, at : at + LANES] = value
        return 0

    for i in range(chunks):
        piece = pl.ds(i * size, size)
        for copy in arrivals[i]:
            copy.wait()
        lax.fori_loop(i * size, (i + 1) * size, subtract, 0)
        for side, chunk, g, row in ((0, 0, 0, 0), (1, chunks - 1, groups - 1, ROWS - 1)):
            if i == chunk:
                for c in range(FIELDS):
                    for z in range(height):
                        k = (side * FIELDS + c) * height + z
                        here = (c, z, g, slice(row, row + 1), slice(None))
                        new[here] = new[here] + edge_rows[k : k + 1, :]
        ends = ((new.at[0, :, piece], density_ref.at[:, piece]), (new.at[1:, :, piece], carried_ref.at[:, :, piece]))
        for k, pair in enumerate(ends):
            departures.append(pltpu.make_async_copy(*pair, out_sems.at[i, k]))
            departures[-1].start()
    for copy in departures:
        copy.wait()


def finish(moved, update, row_layers, cell_layers, chunks=8):
    height, rows, width = update.shape[1:]
    groups = rows // ROWS
    hbm = pl.BlockSpec(memory_space=pltpu.HBM)
    natural = (height, groups, ROWS, width)
    layers = [in_hbm(layer) for layer in row_layers + cell_layers]
    return pl.pallas_call(
        functools.partial(finish_kernel, groups, height, chunks),
        out_shape=[
            jax.ShapeDtypeStruct(natural, jnp.float32),
            jax.ShapeDtypeStruct((FIELDS - 1,) + natural, jnp.float32),
        ],
        in_specs=[hbm] * 10,
        out_specs=[hbm, hbm],
        scratch_shapes=[
            pltpu.VMEM((4,) + row_layers[0].shape, jnp.float32),
            pltpu.VMEM((4,) + cell_layers[0].shape, jnp.float32),
            pltpu.VMEM((groups, height, FIELDS, ROWS, width), jnp.float32),
            pltpu.VMEM((FIELDS,) + natural, jnp.float32),
            pltpu.VMEM((2 * FIELDS * height, width), jnp.float32),
            pltpu.VMEM(cell_layers[0].shape, jnp.float32),
            pltpu.VMEM((FIELDS,) + natural, jnp.float32),
            pltpu.SemaphoreType.DMA((2, 4)),
            pltpu.SemaphoreType.DMA((chunks, 2)),
            pltpu.SemaphoreType.DMA((chunks, 2)),
        ],
        cost_estimate=pl.CostEstimate(flops=moved.size, bytes_accessed=12 * moved.size, transcendentals=0),
        compiler_params=pltpu.CompilerParams(vmem_limit_bytes=20 * 2**20),
        name="finish",
    )(in_hbm(moved.reshape(groups, height, FIELDS, ROWS, width)), in_hbm(update.reshape((FIELDS,) + natural)), *layers)


def flux2(v_left, v_right, speed, q_left, q_right):
    return v_left * q_left + v_right * q_right - speed * (q_right - q_left)


def face_speed(v_left, v_right):
    return jnp.maximum(jnp.abs(v_left), jnp.abs(v_right)) + 1.0


def update_kernel(groups, width, density_ref, carried_ref, o_ref, lower_ref):
    column = lax.broadcasted_iota(jnp.int32, (ROWS, width), 1)
    sub = lax.broadcasted_iota(jnp.int32, (ROWS, width), 0)
    lower_ref[...] = jnp.zeros_like(lower_ref)

    def field(c, z, rows):
        return density_ref[z, rows, :] if c == 0 else carried_ref[c - 1, z, rows, :]

    def body(g, _):
        rows = pl.ds(pl.multiple_of(g * ROWS, ROWS), ROWS)
        after = pl.ds(pl.multiple_of(jnp.minimum(g + 1, groups - 1) * ROWS, ROWS), ROWS)
        inside = jnp.where(g == groups - 1, ROWS - 1, ROWS)
        rho = [field(0, z, rows) for z in range(2)]
        v_height = [field(3, z, rows) / rho[z] for z in range(2)]
        speed_height = 2.0 * face_speed(v_height[0], v_height[1])
        for z in range(2):
            v_r = field(1, z, rows) / rho[z]
            v_a = field(2, z, rows) / rho[z]
            v_r_next = field(1, z, after) / field(0, z, after)
            v_r_up = pltpu.roll(jnp.where(sub == 0, v_r_next, v_r), ROWS - 1, 0)
            speed_r = face_speed(v_r, v_r_up)
            v_a_up = pltpu.roll(v_a, width - 1, 1)
            speed_a = face_speed(v_a, v_a_up)
            for c in range(FIELDS):
                q = field(c, z, rows)
                q_up = pltpu.roll(jnp.where(sub == 0, field(c, z, after), q), ROWS - 1, 0)
                upper = jnp.where(sub < inside, flux2(v_r, v_r_up, speed_r, q, q_up), 0.0)
                lower = pltpu.roll(jnp.where(sub == ROWS - 1, lower_ref[c, z], upper), 1, 0)
                lower_ref[c, z] = upper
                total = upper - lower
                q_up = pltpu.roll(q, width - 1, 1)
                upper = jnp.where(column < width - 1, flux2(v_a, v_a_up, speed_a, q, q_up), 0.0)
                total = total + (upper - pltpu.roll(upper, 1, 1))
                total = total + speed_height * (q - field(c, 1 - z, rows))
                o_ref[c, z, rows, :] = 0.04 * total
        return 0

    lax.fori_loop(0, groups, body, 0)


def update_of(density, carried):
    rows, width = density.shape[1:]
    size = FIELDS * density.size
    vmem = pl.BlockSpec(memory_space=pltpu.VMEM)
    return pl.pallas_call(
        functools.partial(update_kernel, rows // ROWS, width),
        out_shape=pltpu.HBM((FIELDS,) + density.shape, density.dtype),
        in_specs=[vmem] * 2,
        out_specs=vmem,
        scratch_shapes=[pltpu.VMEM((FIELDS, 2, ROWS, width), jnp.float32)],
        cost_estimate=pl.CostEstimate(flops=40 * size, bytes_accessed=8 * size, transcendentals=0),
        compiler_params=pltpu.CompilerParams(vmem_limit_bytes=24 * 2**20),
        name="flux_update",
    )(density, carried)


def border_kernel(groups, height, width, density_ref, carried_ref, first_rows, last_rows, first_cells, last_cells, rows, cells, sems):
    copies = []
    for side, g, at in ((0, 0, 0), (1, groups - 1, width - LANES)):
        for i, (source, fields) in enumerate(((density_ref, 0), (carried_ref, pl.ds(1, FIELDS - 1)))):
            lead = (slice(None),) * (1 + i)
            rest = (slice(None),) * 2
            copies.append(pltpu.make_async_copy(source.at[lead + (g,)], rows.at[side, fields], sems.at[side, i, 0]))
            copies.append(
                pltpu.make_async_copy(
                    source.at[lead + rest + (pl.ds(at, LANES),)], cells.at[side, fields], sems.at[side, i, 1]
                )
            )
    for copy in copies:
        copy.start()
    for copy in copies:
        copy.wait()
    lane = lax.broadcasted_iota(jnp.int32, (ROWS, LANES), 1)
    for side, out, row in ((0, first_rows, 0), (1, last_rows, ROWS - 1)):
        for k in range(FIELDS * height):
            out[k : k + 1, :] = rows[side, k // height, k % height, row : row + 1, :]

    def gather(g, _):
        here = pl.ds(pl.multiple_of(g * ROWS, ROWS), ROWS)
        for side, out, at in ((0, first_cells, 0), (1, last_cells, LANES - 1)):
            total = jnp.zeros((ROWS, LANES), jnp.float32)
            for k in range(FIELDS * height):
                value = pltpu.roll(cells[side, k // height, k % height, g], (k - at) % LANES, 1)
                total = jnp.where(lane == k, value, total)
            out[here, :] = total
        return 0

    lax.fori_loop(0, groups, gather, 0)


def borders_of(density, carried):
    height, rows, width = density.shape
    groups = rows // ROWS
    natural = (height, groups, ROWS, width)
    row_shape = pltpu.HBM((FIELDS * height, width), jnp.float32)
    cell_shape = pltpu.HBM((rows, LANES), jnp.float32)
    return pl.pallas_call(
        functools.partial(border_kernel, groups, height, width),
        out_shape=[row_shape, row_shape, cell_shape, cell_shape],
        in_specs=[pl.BlockSpec(memory_space=pltpu.HBM)] * 2,
        out_specs=[pl.BlockSpec(memory_space=pltpu.VMEM)] * 4,
        scratch_shapes=[
            pltpu.VMEM((2, FIELDS, height, ROWS, width), jnp.float32),
            pltpu.VMEM((2, FIELDS, height, groups, ROWS, LANES), jnp.float32),
            pltpu.SemaphoreType.DMA((2, 2, 2)),
        ],
        compiler_params=pltpu.CompilerParams(vmem_limit_bytes=8 * 2**20),
        name="borders",
    )(in_hbm(density.reshape(natural)), in_hbm(carried.reshape((FIELDS - 1,) + natural)))


def local(density, carried, cycle_shift, cycle_fraction):
    height, rows, width = density.shape
    devices = lax.axis_size("phi")
    packed = pack(density, carried)
    received = lax.all_to_all(
        packed.reshape(devices, FIELDS, ROWS, width), "phi", 0, 0, tiled=True
    )
    moved = shift_rows(received, cycle_shift, cycle_fraction, height)
    moved, density, carried = lax.optimization_barrier((moved, density, carried))
    moved = lax.all_to_all(moved, "phi", 0, 0, tiled=True)

    first_rows, last_rows, first_cells, last_cells = borders_of(density, carried)
    inner = neighbours(last_rows, "rad", 1, False)
    outer = neighbours(first_rows, "rad", -1, False)
    left = neighbours(last_cells, "phi", 1, True)
    right = neighbours(first_cells, "phi", -1, True)
    update = update_of(density, carried)
    density_next, carried_next = finish(
        moved,
        update,
        [inner, first_rows, last_rows, outer],
        [left, first_cells, last_cells, right],
    )
    return density_next.reshape(density.shape), carried_next.reshape(carried.shape)


def solution(mesh):
    placed = (P(None, "rad", "phi"), P(None, None, "rad", "phi"), P("rad"), P("rad"))
    return jax.shard_map(
        local,
        mesh=mesh,
        in_specs=placed,
        out_specs=(P(None, "rad", "phi"), P(None, None, "rad", "phi")),
        check_vma=False,
    )
```

```python
import functools

import jax
import jax.numpy as jnp
from jax import lax
from jax.experimental import pallas as pl
from jax.experimental.pallas import tpu as pltpu
from jax.sharding import PartitionSpec as P

FIELDS = 8
ROWS = 8
LANES = 128


def neighbours(value, axis, step, wrap):
    count = lax.axis_size(axis)
    pairs = [(i, i + step) for i in range(count)]
    if wrap:
        pairs = [(i, j % count) for i, j in pairs]
    else:
        pairs = [(i, j) for i, j in pairs if 0 <= j < count]
    return lax.ppermute(value, axis, pairs)


def in_hbm(value):
    return pltpu.with_memory_space_constraint(value, pltpu.HBM)


def exchanged(registers, sub):
    values = list(registers)
    for k in (4, 2, 1):
        low = (sub & k) == 0
        result = list(values)
        for i in range(ROWS):
            if not i & k:
                a, b = values[i], values[i + k]
                result[i] = jnp.where(low, a, pltpu.roll(b, k, 0))
                result[i + k] = jnp.where(low, pltpu.roll(a, ROWS - k, 0), b)
        values = result
    return values


def pack_kernel(groups, height, chunks, density_ref, carried_ref, o_ref, taken, sems):
    size = groups // chunks
    width = taken.shape[-1]
    sub = lax.broadcasted_iota(jnp.int32, (ROWS, LANES), 0)
    arrivals = []
    for i in range(chunks):
        piece = pl.ds(i * size, size)
        ends = ((density_ref.at[:, piece], taken.at[0, :, piece]), (carried_ref.at[:, :, piece], taken.at[1:, :, piece]))
        arrivals.append([pltpu.make_async_copy(*pair, sems.at[i, k]) for k, pair in enumerate(ends)])
        for copy in arrivals[i]:
            copy.start()

    def reorder(g, _):
        for z in range(height):
            for t in range(width // LANES):
                by_row = exchanged([taken[c, z, g, :, t * LANES : (t + 1) * LANES] for c in range(FIELDS)], sub)
                for row in range(ROWS):
                    o_ref[g * height + z, row, t] = by_row[row]
        return 0

    for i in range(chunks):
        for copy in arrivals[i]:
            copy.wait()
        lax.fori_loop(i * size, (i + 1) * size, reorder, 0, unroll=2)


def pack(density, carried, chunks=4):
    height, rows, width = density.shape
    groups = rows // ROWS
    natural = (height, groups, ROWS, width)
    hbm = pl.BlockSpec(memory_space=pltpu.HBM)
    return pl.pallas_call(
        functools.partial(pack_kernel, groups, height, chunks),
        out_shape=pltpu.VMEM((groups * height, ROWS, width // LANES, FIELDS, LANES), density.dtype),
        in_specs=[hbm, hbm],
        out_specs=pl.BlockSpec(memory_space=pltpu.VMEM),
        scratch_shapes=[pltpu.VMEM((FIELDS,) + natural, jnp.float32), pltpu.SemaphoreType.DMA((chunks, 2))],
        cost_estimate=pl.CostEstimate(flops=0, bytes_accessed=64 * density.size, transcendentals=0),
        compiler_params=pltpu.CompilerParams(vmem_limit_bytes=12 * 2**20),
        name="pack",
    )(in_hbm(density.reshape(natural)), in_hbm(carried.reshape((FIELDS - 1,) + natural)))


def shift_kernel(blocks, tiles, chunks, height, shift_ref, fraction_ref, x_ref, o_ref, placed, out_sems):
    size = blocks // chunks
    tile_bits, skip = tiles.bit_length() - 1, (ROWS - 1) * tiles
    total = blocks * tiles
    lane = lax.broadcasted_iota(jnp.int32, (FIELDS, LANES), 1)
    base = (lax.axis_index("phi") // height) * ROWS
    shifts = [shift_ref[base + row] for row in range(ROWS)]
    whole = [s // LANES for s in shifts]
    part = [s % LANES for s in shifts]
    fraction = [fraction_ref[base + row] for row in range(ROWS)]

    def turned(row, tile):
        source = (tile - whole[row]) & (total - 1)
        return pltpu.roll(x_ref[source + (source >> tile_bits) * skip + row * tiles], part[row], 1)

    def step(tile, row, carry):
        turned_before, moved_before = carry
        now = turned(row, tile)
        first = jnp.where(lane >= part[row], now, turned_before)
        rolled = pltpu.roll(first, 1, 1)
        second = jnp.where(lane >= 1, rolled, moved_before)
        value = (1.0 - fraction[row]) * first + fraction[row] * second
        return value, (now, rolled)

    def place(block, carries):
        carries = list(carries)
        for t in range(tiles):
            for row in range(ROWS):
                placed[block, row, t], carries[row] = step(block * tiles + t, row, carries[row])
        return tuple(carries)

    carries = []
    for row in range(ROWS):
        before = turned(row, -2)
        carries.append(step(-1, row, (before, before))[1])
    carries = tuple(carries)
    departures = []
    for i in range(chunks):
        piece = pl.ds(i * size, size)
        carries = lax.fori_loop(i * size, (i + 1) * size, place, carries, unroll=4)
        departures.append(pltpu.make_async_copy(placed.at[piece], o_ref.at[piece], out_sems.at[i]))
        departures[i].start()
    for copy in departures:
        copy.wait()


def shift_rows(received, shifts, fractions, height, chunks=8):
    blocks, _, tiles, _, _ = received.shape
    smem, hbm = pl.BlockSpec(memory_space=pltpu.SMEM), pl.BlockSpec(memory_space=pltpu.HBM)
    return pl.pallas_call(
        functools.partial(shift_kernel, blocks, tiles, chunks, height),
        out_shape=pltpu.HBM(received.shape, received.dtype),
        in_specs=[smem, smem, pl.BlockSpec(memory_space=pltpu.VMEM)],
        out_specs=hbm,
        scratch_shapes=[pltpu.VMEM(received.shape, jnp.float32), pltpu.SemaphoreType.DMA((chunks,))],
        cost_estimate=pl.CostEstimate(
            flops=8 * received.size, bytes_accessed=8 * received.size, transcendentals=0
        ),
        compiler_params=pltpu.CompilerParams(vmem_limit_bytes=20 * 2**20),
        name="shift_rows",
    )(shifts, fractions, pltpu.with_memory_space_constraint(received.reshape(-1, FIELDS, LANES), pltpu.VMEM))


def edge_fluxes(height, inner, first_rows, last_rows, outer, left, first_cells, last_cells, right, rows_ref, cells_ref):
    def layer(ref, c):
        return ref[c * height : (c + 1) * height, :]

    def radial(ref):
        rho = layer(ref, 0)
        return layer(ref, 1) / jnp.where(rho == 0.0, 1.0, rho)

    for lower, upper, sign, start in ((inner, first_rows, 0.04, 0), (last_rows, outer, -0.04, FIELDS * height)):
        v_lower, v_upper = radial(lower), radial(upper)
        speed = face_speed(v_lower, v_upper)
        for c in range(FIELDS):
            flux = flux2(v_lower, v_upper, speed, layer(lower, c), layer(upper, c))
            rows_ref[start + c * height : start + (c + 1) * height, :] = sign * flux

    odd = lax.broadcasted_iota(jnp.int32, cells_ref.shape, 1) % 2 == 1

    def azimuthal(cells):
        v = [cells[:, 4 + z : 5 + z] / cells[:, z : z + 1] for z in range(2)]
        return jnp.where(odd, v[1], v[0])

    def flux(lower, upper):
        v_lower, v_upper = azimuthal(lower), azimuthal(upper)
        return 0.04 * flux2(v_lower, v_upper, face_speed(v_lower, v_upper), lower, upper)

    upper_faces = pltpu.roll(flux(last_cells[...], right[...]), FIELDS * height, 1)
    cells_ref[...] = flux(left[...], first_cells[...]) - upper_faces


def finish_kernel(
    groups,
    height,
    chunks,
    moved_ref,
    update_ref,
    *refs,
):
    row_refs, cell_refs = refs[:4], refs[4:8]
    density_ref, carried_ref, layer_rows, layer_cells, taken, change, edge_rows, edge_cells, new = refs[8:17]
    edge_sems, in_sems, out_sems = refs[17:]
    size = groups // chunks
    width = change.shape[-1]
    lane = lax.broadcasted_iota(jnp.int32, (ROWS, LANES), 1)
    sub = lax.broadcasted_iota(jnp.int32, (ROWS, LANES), 0)
    edges = []
    for i in range(4):
        edges.append(pltpu.make_async_copy(row_refs[i], layer_rows.at[i], edge_sems.at[0, i]))
        edges.append(pltpu.make_async_copy(cell_refs[i], layer_cells.at[i], edge_sems.at[1, i]))
    for copy in edges:
        copy.start()
    arrivals, departures = [], []
    for i in range(chunks):
        piece = pl.ds(i * size, size)
        ends = ((moved_ref.at[piece], taken.at[piece]), (update_ref.at[:, :, piece], change.at[:, :, piece]))
        arrivals.append([pltpu.make_async_copy(*pair, in_sems.at[i, k]) for k, pair in enumerate(ends)])
        for copy in arrivals[i]:
            copy.start()
    for copy in edges:
        copy.wait()
    layers = [layer_rows.at[i] for i in range(4)] + [layer_cells.at[i] for i in range(4)]
    edge_fluxes(height, *layers, edge_rows, edge_cells)

    def subtract(g, _):
        cells = edge_cells[pl.ds(pl.multiple_of(g * ROWS, ROWS), ROWS), :]
        for z in range(height):
            for t in range(width // LANES):
                at = t * LANES
                by_field = exchanged([taken[g, z, row, t] for row in range(ROWS)], sub)
                for c in range(FIELDS):
                    k = c * height + z
                    value = by_field[c] - change[c, z, g, :, at : at + LANES]
                    if at == 0:
                        value = value + jnp.where(lane == 0, cells[:, k : k + 1], 0.0)
                    if at == width - LANES:
                        m = FIELDS * height + k
                        value = value + jnp.where(lane == LANES - 1, cells[:, m : m + 1], 0.0)
                    new[c, z, g, :, at : at + LANES] = value
        return 0

    for i in range(chunks):
        piece = pl.ds(i * size, size)
        for copy in arrivals[i]:
            copy.wait()
        lax.fori_loop(i * size, (i + 1) * size, subtract, 0, unroll=4)
        for side, chunk, g, row in ((0, 0, 0, 0), (1, chunks - 1, groups - 1, ROWS - 1)):
            if i == chunk:
                for c in range(FIELDS):
                    for z in range(height):
                        k = (side * FIELDS + c) * height + z
                        here = (c, z, g, slice(row, row + 1), slice(None))
                        new[here] = new[here] + edge_rows[k : k + 1, :]
        ends = ((new.at[0, :, piece], density_ref.at[:, piece]), (new.at[1:, :, piece], carried_ref.at[:, :, piece]))
        for k, pair in enumerate(ends):
            departures.append(pltpu.make_async_copy(*pair, out_sems.at[i, k]))
            departures[-1].start()
    for copy in departures:
        copy.wait()


def finish(moved, update, row_layers, cell_layers, chunks=4):
    height, rows, width = update.shape[1:]
    groups = rows // ROWS
    hbm = pl.BlockSpec(memory_space=pltpu.HBM)
    natural = (height, groups, ROWS, width)
    layers = [in_hbm(layer) for layer in row_layers + cell_layers]
    return pl.pallas_call(
        functools.partial(finish_kernel, groups, height, chunks),
        out_shape=[
            jax.ShapeDtypeStruct(natural, jnp.float32),
            jax.ShapeDtypeStruct((FIELDS - 1,) + natural, jnp.float32),
        ],
        in_specs=[hbm] * 10,
        out_specs=[hbm, hbm],
        scratch_shapes=[
            pltpu.VMEM((4,) + row_layers[0].shape, jnp.float32),
            pltpu.VMEM((4,) + cell_layers[0].shape, jnp.float32),
            pltpu.VMEM((groups, height) + moved.shape[1:], jnp.float32),
            pltpu.VMEM((FIELDS,) + natural, jnp.float32),
            pltpu.VMEM((2 * FIELDS * height, width), jnp.float32),
            pltpu.VMEM(cell_layers[0].shape, jnp.float32),
            pltpu.VMEM((FIELDS,) + natural, jnp.float32),
            pltpu.SemaphoreType.DMA((2, 4)),
            pltpu.SemaphoreType.DMA((chunks, 2)),
            pltpu.SemaphoreType.DMA((chunks, 2)),
        ],
        cost_estimate=pl.CostEstimate(flops=moved.size, bytes_accessed=12 * moved.size, transcendentals=0),
        compiler_params=pltpu.CompilerParams(vmem_limit_bytes=20 * 2**20),
        name="finish",
    )(in_hbm(moved.reshape((groups, height) + moved.shape[1:])), in_hbm(update.reshape((FIELDS,) + natural)), *layers)


def flux2(v_left, v_right, speed, q_left, q_right):
    return v_left * q_left + v_right * q_right - speed * (q_right - q_left)


def face_speed(v_left, v_right):
    return jnp.maximum(jnp.abs(v_left), jnp.abs(v_right)) + 1.0


def update_kernel(groups, width, density_ref, carried_ref, o_ref, lower_ref):
    column = lax.broadcasted_iota(jnp.int32, (ROWS, width), 1)
    sub = lax.broadcasted_iota(jnp.int32, (ROWS, width), 0)
    lower_ref[...] = jnp.zeros_like(lower_ref)

    def field(c, z, rows):
        return density_ref[z, rows, :] if c == 0 else carried_ref[c - 1, z, rows, :]

    def body(g, _):
        rows = pl.ds(pl.multiple_of(g * ROWS, ROWS), ROWS)
        after = pl.ds(pl.multiple_of(jnp.minimum(g + 1, groups - 1) * ROWS, ROWS), ROWS)
        inside = jnp.where(g == groups - 1, ROWS - 1, ROWS)
        rho = [field(0, z, rows) for z in range(2)]
        v_height = [field(3, z, rows) / rho[z] for z in range(2)]
        speed_height = 2.0 * face_speed(v_height[0], v_height[1])
        for z in range(2):
            v_r = field(1, z, rows) / rho[z]
            v_a = field(2, z, rows) / rho[z]
            v_r_next = field(1, z, after) / field(0, z, after)
            v_r_up = pltpu.roll(jnp.where(sub == 0, v_r_next, v_r), ROWS - 1, 0)
            speed_r = face_speed(v_r, v_r_up)
            v_a_up = pltpu.roll(v_a, width - 1, 1)
            speed_a = face_speed(v_a, v_a_up)
            for c in range(FIELDS):
                q = field(c, z, rows)
                q_up = pltpu.roll(jnp.where(sub == 0, field(c, z, after), q), ROWS - 1, 0)
                upper = jnp.where(sub < inside, flux2(v_r, v_r_up, speed_r, q, q_up), 0.0)
                lower = pltpu.roll(jnp.where(sub == ROWS - 1, lower_ref[c, z], upper), 1, 0)
                lower_ref[c, z] = upper
                total = upper - lower
                q_up = pltpu.roll(q, width - 1, 1)
                upper = jnp.where(column < width - 1, flux2(v_a, v_a_up, speed_a, q, q_up), 0.0)
                total = total + (upper - pltpu.roll(upper, 1, 1))
                total = total + speed_height * (q - field(c, 1 - z, rows))
                o_ref[c, z, rows, :] = 0.04 * total
        return 0

    lax.fori_loop(0, groups, body, 0)


def update_of(density, carried):
    rows, width = density.shape[1:]
    size = FIELDS * density.size
    vmem = pl.BlockSpec(memory_space=pltpu.VMEM)
    return pl.pallas_call(
        functools.partial(update_kernel, rows // ROWS, width),
        out_shape=pltpu.HBM((FIELDS,) + density.shape, density.dtype),
        in_specs=[vmem] * 2,
        out_specs=vmem,
        scratch_shapes=[pltpu.VMEM((FIELDS, 2, ROWS, width), jnp.float32)],
        cost_estimate=pl.CostEstimate(flops=40 * size, bytes_accessed=8 * size, transcendentals=0),
        compiler_params=pltpu.CompilerParams(vmem_limit_bytes=24 * 2**20),
        name="flux_update",
    )(density, carried)


def border_kernel(groups, height, width, density_ref, carried_ref, first_rows, last_rows, first_cells, last_cells, rows, cells, sems):
    copies = []
    for side, g, at in ((0, 0, 0), (1, groups - 1, width - LANES)):
        for i, (source, fields) in enumerate(((density_ref, 0), (carried_ref, pl.ds(1, FIELDS - 1)))):
            lead = (slice(None),) * (1 + i)
            rest = (slice(None),) * 2
            copies.append(pltpu.make_async_copy(source.at[lead + (g,)], rows.at[side, fields], sems.at[side, i, 0]))
            copies.append(
                pltpu.make_async_copy(
                    source.at[lead + rest + (pl.ds(at, LANES),)], cells.at[side, fields], sems.at[side, i, 1]
                )
            )
    for copy in copies:
        copy.start()
    for copy in copies:
        copy.wait()
    lane = lax.broadcasted_iota(jnp.int32, (ROWS, LANES), 1)
    for side, out, row in ((0, first_rows, 0), (1, last_rows, ROWS - 1)):
        for k in range(FIELDS * height):
            out[k : k + 1, :] = rows[side, k // height, k % height, row : row + 1, :]

    def gather(g, _):
        here = pl.ds(pl.multiple_of(g * ROWS, ROWS), ROWS)
        for side, out, at in ((0, first_cells, 0), (1, last_cells, LANES - 1)):
            total = jnp.zeros((ROWS, LANES), jnp.float32)
            for k in range(FIELDS * height):
                value = pltpu.roll(cells[side, k // height, k % height, g], (k - at) % LANES, 1)
                total = jnp.where(lane == k, value, total)
            out[here, :] = total
        return 0

    lax.fori_loop(0, groups, gather, 0)


def borders_of(density, carried):
    height, rows, width = density.shape
    groups = rows // ROWS
    natural = (height, groups, ROWS, width)
    row_shape = pltpu.HBM((FIELDS * height, width), jnp.float32)
    cell_shape = pltpu.HBM((rows, LANES), jnp.float32)
    return pl.pallas_call(
        functools.partial(border_kernel, groups, height, width),
        out_shape=[row_shape, row_shape, cell_shape, cell_shape],
        in_specs=[pl.BlockSpec(memory_space=pltpu.HBM)] * 2,
        out_specs=[pl.BlockSpec(memory_space=pltpu.VMEM)] * 4,
        scratch_shapes=[
            pltpu.VMEM((2, FIELDS, height, ROWS, width), jnp.float32),
            pltpu.VMEM((2, FIELDS, height, groups, ROWS, LANES), jnp.float32),
            pltpu.SemaphoreType.DMA((2, 2, 2)),
        ],
        compiler_params=pltpu.CompilerParams(vmem_limit_bytes=8 * 2**20),
        name="borders",
    )(in_hbm(density.reshape(natural)), in_hbm(carried.reshape((FIELDS - 1,) + natural)))


def local(density, carried, cycle_shift, cycle_fraction):
    height = density.shape[0]
    received = lax.all_to_all(pack(density, carried), "phi", 0, 0, tiled=True)
    moved = shift_rows(received, cycle_shift, cycle_fraction, height)
    moved, density, carried = lax.optimization_barrier((moved, density, carried))
    moved = lax.all_to_all(moved, "phi", 0, 0, tiled=True)

    first_rows, last_rows, first_cells, last_cells = borders_of(density, carried)
    inner = neighbours(last_rows, "rad", 1, False)
    outer = neighbours(first_rows, "rad", -1, False)
    left = neighbours(last_cells, "phi", 1, True)
    right = neighbours(first_cells, "phi", -1, True)
    update = update_of(density, carried)
    density_next, carried_next = finish(
        moved,
        update,
        [inner, first_rows, last_rows, outer],
        [left, first_cells, last_cells, right],
    )
    return density_next.reshape(density.shape), carried_next.reshape(carried.shape)


def solution(mesh):
    placed = (P(None, "rad", "phi"), P(None, None, "rad", "phi"), P("rad"), P("rad"))
    return jax.shard_map(
        local,
        mesh=mesh,
        in_specs=placed,
        out_specs=(P(None, "rad", "phi"), P(None, None, "rad", "phi")),
        check_vma=False,
    )
```

```python
import functools

import jax
import jax.numpy as jnp
from jax import lax
from jax.experimental import pallas as pl
from jax.experimental.pallas import tpu as pltpu
from jax.sharding import PartitionSpec as P

FIELDS = 8
ROWS = 8
LANES = 128


def neighbours(value, axis, step, wrap):
    count = lax.axis_size(axis)
    pairs = [(i, i + step) for i in range(count)]
    if wrap:
        pairs = [(i, j % count) for i, j in pairs]
    else:
        pairs = [(i, j) for i, j in pairs if 0 <= j < count]
    return lax.ppermute(value, axis, pairs)


def in_hbm(value):
    return pltpu.with_memory_space_constraint(value, pltpu.HBM)


def exchanged(registers, sub):
    values = list(registers)
    for k in (4, 2, 1):
        low = (sub & k) == 0
        result = list(values)
        for i in range(ROWS):
            if not i & k:
                a, b = values[i], values[i + k]
                result[i] = jnp.where(low, a, pltpu.roll(b, k, 0))
                result[i + k] = jnp.where(low, pltpu.roll(a, ROWS - k, 0), b)
        values = result
    return values


def pack_kernel(groups, height, chunks, density_ref, carried_ref, o_ref, taken, sems):
    size = groups // chunks
    width = taken.shape[-1]
    sub = lax.broadcasted_iota(jnp.int32, (ROWS, LANES), 0)
    arrivals = []
    for i in range(chunks):
        piece = pl.ds(i * size, size)
        ends = ((density_ref.at[:, piece], taken.at[0, :, piece]), (carried_ref.at[:, :, piece], taken.at[1:, :, piece]))
        arrivals.append([pltpu.make_async_copy(*pair, sems.at[i, k]) for k, pair in enumerate(ends)])
        for copy in arrivals[i]:
            copy.start()

    def reorder(g, _):
        for z in range(height):
            for t in range(width // LANES):
                by_row = exchanged([taken[c, z, g, :, t * LANES : (t + 1) * LANES] for c in range(FIELDS)], sub)
                for row in range(ROWS):
                    o_ref[g * height + z, row, t] = by_row[row]
        return 0

    for i in range(chunks):
        for copy in arrivals[i]:
            copy.wait()
        lax.fori_loop(i * size, (i + 1) * size, reorder, 0, unroll=2)


def pack(density, carried, chunks=4):
    height, rows, width = density.shape
    groups = rows // ROWS
    natural = (height, groups, ROWS, width)
    hbm = pl.BlockSpec(memory_space=pltpu.HBM)
    return pl.pallas_call(
        functools.partial(pack_kernel, groups, height, chunks),
        out_shape=pltpu.VMEM((groups * height, ROWS, width // LANES, FIELDS, LANES), density.dtype),
        in_specs=[hbm, hbm],
        out_specs=pl.BlockSpec(memory_space=pltpu.VMEM),
        scratch_shapes=[pltpu.VMEM((FIELDS,) + natural, jnp.float32), pltpu.SemaphoreType.DMA((chunks, 2))],
        cost_estimate=pl.CostEstimate(flops=0, bytes_accessed=64 * density.size, transcendentals=0),
        compiler_params=pltpu.CompilerParams(vmem_limit_bytes=12 * 2**20),
        name="pack",
    )(in_hbm(density.reshape(natural)), in_hbm(carried.reshape((FIELDS - 1,) + natural)))


def shift_kernel(blocks, tiles, chunks, height, shift_ref, fraction_ref, x_ref, o_ref, placed, out_sems):
    size = blocks // chunks
    tile_bits, skip = tiles.bit_length() - 1, (ROWS - 1) * tiles
    total = blocks * tiles
    lane = lax.broadcasted_iota(jnp.int32, (FIELDS, LANES), 1)
    base = (lax.axis_index("phi") // height) * ROWS
    shifts = [shift_ref[base + row] for row in range(ROWS)]
    whole = [s // LANES for s in shifts]
    part = [s % LANES for s in shifts]
    fraction = [fraction_ref[base + row] for row in range(ROWS)]

    def turned(row, tile):
        source = (tile - whole[row]) & (total - 1)
        return pltpu.roll(x_ref[source + (source >> tile_bits) * skip + row * tiles], part[row], 1)

    def step(tile, row, carry):
        turned_before, moved_before = carry
        now = turned(row, tile)
        first = jnp.where(lane >= part[row], now, turned_before)
        rolled = pltpu.roll(first, 1, 1)
        second = jnp.where(lane >= 1, rolled, moved_before)
        value = (1.0 - fraction[row]) * first + fraction[row] * second
        return value, (now, rolled)

    def place(block, carries):
        carries = list(carries)
        for t in range(tiles):
            for row in range(ROWS):
                placed[block, row, t], carries[row] = step(block * tiles + t, row, carries[row])
        return tuple(carries)

    carries = []
    for row in range(ROWS):
        before = turned(row, -2)
        carries.append(step(-1, row, (before, before))[1])
    carries = tuple(carries)
    departures = []
    for i in range(chunks):
        piece = pl.ds(i * size, size)
        carries = lax.fori_loop(i * size, (i + 1) * size, place, carries, unroll=4)
        departures.append(pltpu.make_async_copy(placed.at[piece], o_ref.at[piece], out_sems.at[i]))
        departures[i].start()
    for copy in departures:
        copy.wait()


def shift_rows(received, shifts, fractions, height, chunks=8):
    blocks, _, tiles, _, _ = received.shape
    smem, hbm = pl.BlockSpec(memory_space=pltpu.SMEM), pl.BlockSpec(memory_space=pltpu.HBM)
    return pl.pallas_call(
        functools.partial(shift_kernel, blocks, tiles, chunks, height),
        out_shape=pltpu.HBM(received.shape, received.dtype),
        in_specs=[smem, smem, pl.BlockSpec(memory_space=pltpu.VMEM)],
        out_specs=hbm,
        scratch_shapes=[pltpu.VMEM(received.shape, jnp.float32), pltpu.SemaphoreType.DMA((chunks,))],
        cost_estimate=pl.CostEstimate(
            flops=8 * received.size, bytes_accessed=8 * received.size, transcendentals=0
        ),
        compiler_params=pltpu.CompilerParams(vmem_limit_bytes=20 * 2**20),
        name="shift_rows",
    )(shifts, fractions, pltpu.with_memory_space_constraint(received.reshape(-1, FIELDS, LANES), pltpu.VMEM))


def edge_fluxes(height, inner, first_rows, last_rows, outer, left, first_cells, last_cells, right, rows_ref, cells_ref):
    def layer(ref, c):
        return ref[c * height : (c + 1) * height, :]

    def velocity(ref, direction):
        rho = layer(ref, 0)
        return layer(ref, 1 + direction) / jnp.where(rho == 0.0, 1.0, rho)

    def fluxes(lower, upper, direction, scale, out, start):
        v_lower, v_upper = velocity(lower, direction), velocity(upper, direction)
        speed = face_speed(v_lower, v_upper)
        for c in range(FIELDS):
            flux = flux2(v_lower, v_upper, speed, layer(lower, c), layer(upper, c))
            out[start + c * height : start + (c + 1) * height, :] = scale * flux

    fluxes(inner, first_rows, 0, 0.04, rows_ref, 0)
    fluxes(last_rows, outer, 0, -0.04, rows_ref, FIELDS * height)
    fluxes(left, first_cells, 1, 0.04, cells_ref, 0)
    fluxes(last_cells, right, 1, -0.04, cells_ref, FIELDS * height)


def finish_kernel(
    groups,
    height,
    chunks,
    moved_ref,
    update_ref,
    *refs,
):
    row_refs, cell_refs = refs[:4], refs[4:8]
    density_ref, carried_ref, layer_rows, layer_cells, taken, change, edge_rows, edge_cells, new = refs[8:17]
    edge_sems, in_sems, out_sems = refs[17:]
    size = groups // chunks
    width = change.shape[-1]
    lane = lax.broadcasted_iota(jnp.int32, (ROWS, LANES), 1)
    sub = lax.broadcasted_iota(jnp.int32, (ROWS, LANES), 0)
    edges = []
    for i in range(4):
        edges.append(pltpu.make_async_copy(row_refs[i], layer_rows.at[i], edge_sems.at[0, i]))
        edges.append(pltpu.make_async_copy(cell_refs[i], layer_cells.at[i], edge_sems.at[1, i]))
    for copy in edges:
        copy.start()
    arrivals, departures = [], []
    for i in range(chunks):
        piece = pl.ds(i * size, size)
        ends = ((moved_ref.at[piece], taken.at[piece]), (update_ref.at[:, :, piece], change.at[:, :, piece]))
        arrivals.append([pltpu.make_async_copy(*pair, in_sems.at[i, k]) for k, pair in enumerate(ends)])
        for copy in arrivals[i]:
            copy.start()
    for copy in edges:
        copy.wait()
    layers = [layer_rows.at[i] for i in range(4)] + [layer_cells.at[i] for i in range(4)]
    edge_cells[2 * FIELDS * height :, :] = jnp.zeros(
        (LANES - 2 * FIELDS * height, edge_cells.shape[1]), jnp.float32
    )
    edge_fluxes(height, *layers, edge_rows, edge_cells)
    edge_cells[...] = edge_cells[...].T

    def subtract(g, _):
        cells = edge_cells[pl.ds(pl.multiple_of(g * ROWS, ROWS), ROWS), :]
        for z in range(height):
            for t in range(width // LANES):
                at = t * LANES
                by_field = exchanged([taken[g, z, row, t] for row in range(ROWS)], sub)
                for c in range(FIELDS):
                    k = c * height + z
                    value = by_field[c] - change[c, z, g, :, at : at + LANES]
                    if at == 0:
                        value = value + jnp.where(lane == 0, cells[:, k : k + 1], 0.0)
                    if at == width - LANES:
                        m = FIELDS * height + k
                        value = value + jnp.where(lane == LANES - 1, cells[:, m : m + 1], 0.0)
                    new[c, z, g, :, at : at + LANES] = value
        return 0

    for i in range(chunks):
        piece = pl.ds(i * size, size)
        for copy in arrivals[i]:
            copy.wait()
        lax.fori_loop(i * size, (i + 1) * size, subtract, 0, unroll=4)
        for side, chunk, g, row in ((0, 0, 0, 0), (1, chunks - 1, groups - 1, ROWS - 1)):
            if i == chunk:
                for c in range(FIELDS):
                    for z in range(height):
                        k = (side * FIELDS + c) * height + z
                        here = (c, z, g, slice(row, row + 1), slice(None))
                        new[here] = new[here] + edge_rows[k : k + 1, :]
        ends = ((new.at[0, :, piece], density_ref.at[:, piece]), (new.at[1:, :, piece], carried_ref.at[:, :, piece]))
        for k, pair in enumerate(ends):
            departures.append(pltpu.make_async_copy(*pair, out_sems.at[i, k]))
            departures[-1].start()
    for copy in departures:
        copy.wait()


def finish(moved, update, row_layers, cell_layers, chunks=4):
    height, rows, width = update.shape[1:]
    groups = rows // ROWS
    hbm = pl.BlockSpec(memory_space=pltpu.HBM)
    natural = (height, groups, ROWS, width)
    layers = row_layers + cell_layers
    return pl.pallas_call(
        functools.partial(finish_kernel, groups, height, chunks),
        out_shape=[
            jax.ShapeDtypeStruct(natural, jnp.float32),
            jax.ShapeDtypeStruct((FIELDS - 1,) + natural, jnp.float32),
        ],
        in_specs=[hbm] * 2 + [pl.BlockSpec(memory_space=pl.ANY)] * 8,
        out_specs=[hbm, hbm],
        scratch_shapes=[
            pltpu.VMEM((4,) + row_layers[0].shape, jnp.float32),
            pltpu.VMEM((4,) + cell_layers[0].shape, jnp.float32),
            pltpu.VMEM((groups, height) + moved.shape[1:], jnp.float32),
            pltpu.VMEM((FIELDS,) + natural, jnp.float32),
            pltpu.VMEM((2 * FIELDS * height, width), jnp.float32),
            pltpu.VMEM((LANES, rows), jnp.float32),
            pltpu.VMEM((FIELDS,) + natural, jnp.float32),
            pltpu.SemaphoreType.DMA((2, 4)),
            pltpu.SemaphoreType.DMA((chunks, 2)),
            pltpu.SemaphoreType.DMA((chunks, 2)),
        ],
        cost_estimate=pl.CostEstimate(flops=moved.size, bytes_accessed=12 * moved.size, transcendentals=0),
        compiler_params=pltpu.CompilerParams(vmem_limit_bytes=20 * 2**20),
        name="finish",
    )(in_hbm(moved.reshape((groups, height) + moved.shape[1:])), in_hbm(update.reshape((FIELDS,) + natural)), *layers)


def flux2(v_left, v_right, speed, q_left, q_right):
    return v_left * q_left + v_right * q_right - speed * (q_right - q_left)


def face_speed(v_left, v_right):
    return jnp.maximum(jnp.abs(v_left), jnp.abs(v_right)) + 1.0


def update_kernel(groups, width, density_ref, carried_ref, o_ref, lower_ref):
    column = lax.broadcasted_iota(jnp.int32, (ROWS, width), 1)
    sub = lax.broadcasted_iota(jnp.int32, (ROWS, width), 0)
    lower_ref[...] = jnp.zeros_like(lower_ref)

    def field(c, z, rows):
        return density_ref[z, rows, :] if c == 0 else carried_ref[c - 1, z, rows, :]

    def body(g, _):
        rows = pl.ds(pl.multiple_of(g * ROWS, ROWS), ROWS)
        after = pl.ds(pl.multiple_of(jnp.minimum(g + 1, groups - 1) * ROWS, ROWS), ROWS)
        inside = jnp.where(g == groups - 1, ROWS - 1, ROWS)
        rho = [field(0, z, rows) for z in range(2)]
        v_height = [field(3, z, rows) / rho[z] for z in range(2)]
        speed_height = 2.0 * face_speed(v_height[0], v_height[1])
        for z in range(2):
            v_r = field(1, z, rows) / rho[z]
            v_a = field(2, z, rows) / rho[z]
            v_r_next = field(1, z, after) / field(0, z, after)
            v_r_up = pltpu.roll(jnp.where(sub == 0, v_r_next, v_r), ROWS - 1, 0)
            speed_r = face_speed(v_r, v_r_up)
            v_a_up = pltpu.roll(v_a, width - 1, 1)
            speed_a = face_speed(v_a, v_a_up)
            for c in range(FIELDS):
                q = field(c, z, rows)
                q_up = pltpu.roll(jnp.where(sub == 0, field(c, z, after), q), ROWS - 1, 0)
                upper = jnp.where(sub < inside, flux2(v_r, v_r_up, speed_r, q, q_up), 0.0)
                lower = pltpu.roll(jnp.where(sub == ROWS - 1, lower_ref[c, z], upper), 1, 0)
                lower_ref[c, z] = upper
                total = upper - lower
                q_up = pltpu.roll(q, width - 1, 1)
                upper = jnp.where(column < width - 1, flux2(v_a, v_a_up, speed_a, q, q_up), 0.0)
                total = total + (upper - pltpu.roll(upper, 1, 1))
                total = total + speed_height * (q - field(c, 1 - z, rows))
                o_ref[c, z, rows, :] = 0.04 * total
        return 0

    lax.fori_loop(0, groups, body, 0)


def update_of(density, carried):
    rows, width = density.shape[1:]
    size = FIELDS * density.size
    vmem = pl.BlockSpec(memory_space=pltpu.VMEM)
    return pl.pallas_call(
        functools.partial(update_kernel, rows // ROWS, width),
        out_shape=pltpu.HBM((FIELDS,) + density.shape, density.dtype),
        in_specs=[vmem] * 2,
        out_specs=vmem,
        scratch_shapes=[pltpu.VMEM((FIELDS, 2, ROWS, width), jnp.float32)],
        cost_estimate=pl.CostEstimate(flops=40 * size, bytes_accessed=8 * size, transcendentals=0),
        compiler_params=pltpu.CompilerParams(vmem_limit_bytes=24 * 2**20),
        name="flux_update",
    )(density, carried)


def border_kernel(groups, height, width, density_ref, carried_ref, first_rows, last_rows, first_cells, last_cells, rows, cells, columns, sems):
    copies = []
    for side, g, at in ((0, 0, 0), (1, groups - 1, width - LANES)):
        for i, (source, fields) in enumerate(((density_ref, 0), (carried_ref, pl.ds(1, FIELDS - 1)))):
            lead = (slice(None),) * (1 + i)
            rest = (slice(None),) * 2
            copies.append(pltpu.make_async_copy(source.at[lead + (g,)], rows.at[side, fields], sems.at[side, i, 0]))
            copies.append(
                pltpu.make_async_copy(
                    source.at[lead + rest + (pl.ds(at, LANES),)], cells.at[side, fields], sems.at[side, i, 1]
                )
            )
    for copy in copies:
        copy.start()
    for copy in copies:
        copy.wait()
    lane = lax.broadcasted_iota(jnp.int32, (ROWS, LANES), 1)
    for side, out, row in ((0, first_rows, 0), (1, last_rows, ROWS - 1)):
        for k in range(FIELDS * height):
            out[k : k + 1, :] = rows[side, k // height, k % height, row : row + 1, :]

    def gather(g, _):
        here = pl.ds(pl.multiple_of(g * ROWS, ROWS), ROWS)
        for side, at in ((0, 0), (1, LANES - 1)):
            total = jnp.zeros((ROWS, LANES), jnp.float32)
            for k in range(FIELDS * height):
                value = pltpu.roll(cells[side, k // height, k % height, g], (k - at) % LANES, 1)
                total = jnp.where(lane == k, value, total)
            columns[side, here, :] = total
        return 0

    lax.fori_loop(0, groups, gather, 0)
    first_cells[...] = columns[0].T[: FIELDS * height]
    last_cells[...] = columns[1].T[: FIELDS * height]


def borders_of(density, carried):
    height, rows, width = density.shape
    groups = rows // ROWS
    natural = (height, groups, ROWS, width)
    row_shape = pltpu.HBM((FIELDS * height, width), jnp.float32)
    cell_shape = pltpu.HBM((FIELDS * height, rows), jnp.float32)
    return pl.pallas_call(
        functools.partial(border_kernel, groups, height, width),
        out_shape=[row_shape, row_shape, cell_shape, cell_shape],
        in_specs=[pl.BlockSpec(memory_space=pltpu.HBM)] * 2,
        out_specs=[pl.BlockSpec(memory_space=pltpu.VMEM)] * 4,
        scratch_shapes=[
            pltpu.VMEM((2, FIELDS, height, ROWS, width), jnp.float32),
            pltpu.VMEM((2, FIELDS, height, groups, ROWS, LANES), jnp.float32),
            pltpu.VMEM((2, rows, LANES), jnp.float32),
            pltpu.SemaphoreType.DMA((2, 2, 2)),
        ],
        compiler_params=pltpu.CompilerParams(vmem_limit_bytes=8 * 2**20),
        name="borders",
    )(in_hbm(density.reshape(natural)), in_hbm(carried.reshape((FIELDS - 1,) + natural)))


def local(density, carried, cycle_shift, cycle_fraction):
    height = density.shape[0]
    received = lax.all_to_all(pack(density, carried), "phi", 0, 0, tiled=True)
    moved = shift_rows(received, cycle_shift, cycle_fraction, height)
    moved, density, carried = lax.optimization_barrier((moved, density, carried))
    moved = lax.all_to_all(moved, "phi", 0, 0, tiled=True)

    first_rows, last_rows, first_cells, last_cells = borders_of(density, carried)
    inner = neighbours(last_rows, "rad", 1, False)
    outer = neighbours(first_rows, "rad", -1, False)
    left = neighbours(last_cells, "phi", 1, True)
    right = neighbours(first_cells, "phi", -1, True)
    update = update_of(density, carried)
    density_next, carried_next = finish(
        moved,
        update,
        [inner, first_rows, last_rows, outer],
        [left, first_cells, last_cells, right],
    )
    return density_next.reshape(density.shape), carried_next.reshape(carried.shape)


def solution(mesh):
    placed = (P(None, "rad", "phi"), P(None, None, "rad", "phi"), P("rad"), P("rad"))
    return jax.shard_map(
        local,
        mesh=mesh,
        in_specs=placed,
        out_specs=(P(None, "rad", "phi"), P(None, None, "rad", "phi")),
        check_vma=False,
    )
```

```python
import functools

import jax
import jax.numpy as jnp
from jax import lax
from jax.experimental import pallas as pl
from jax.experimental.pallas import tpu as pltpu
from jax.sharding import PartitionSpec as P

FIELDS = 8
ROWS = 8
LANES = 128
NEAR = 6


def neighbours(value, axis, step, wrap):
    count = lax.axis_size(axis)
    pairs = [(i, i + step) for i in range(count)]
    if wrap:
        pairs = [(i, j % count) for i, j in pairs]
    else:
        pairs = [(i, j) for i, j in pairs if 0 <= j < count]
    return lax.ppermute(value, axis, pairs)


def in_hbm(value):
    return pltpu.with_memory_space_constraint(value, pltpu.HBM)


def exchanged(registers, sub):
    values = list(registers)
    for k in (4, 2, 1):
        low = (sub & k) == 0
        result = list(values)
        for i in range(ROWS):
            if not i & k:
                a, b = values[i], values[i + k]
                result[i] = jnp.where(low, a, pltpu.roll(b, k, 0))
                result[i + k] = jnp.where(low, pltpu.roll(a, ROWS - k, 0), b)
        values = result
    return values


def pack_kernel(groups, height, chunks, density_ref, carried_ref, o_ref, taken, sems):
    size = groups // chunks
    width = taken.shape[-1]
    sub = lax.broadcasted_iota(jnp.int32, (ROWS, LANES), 0)
    arrivals = []
    for i in range(chunks):
        piece = pl.ds(i * size, size)
        ends = ((density_ref.at[:, piece], taken.at[0, :, piece]), (carried_ref.at[:, :, piece], taken.at[1:, :, piece]))
        arrivals.append([pltpu.make_async_copy(*pair, sems.at[i, k]) for k, pair in enumerate(ends)])
        for copy in arrivals[i]:
            copy.start()

    def reorder(g, _):
        for z in range(height):
            for t in range(width // LANES):
                by_row = exchanged([taken[c, z, g, :, t * LANES : (t + 1) * LANES] for c in range(FIELDS)], sub)
                for row in range(ROWS):
                    o_ref[g * height + z, row, t] = by_row[row]
        return 0

    for i in range(chunks):
        for copy in arrivals[i]:
            copy.wait()
        lax.fori_loop(i * size, (i + 1) * size, reorder, 0, unroll=2)


def pack(density, carried, chunks=4):
    height, rows, width = density.shape
    groups = rows // ROWS
    natural = (height, groups, ROWS, width)
    hbm = pl.BlockSpec(memory_space=pltpu.HBM)
    return pl.pallas_call(
        functools.partial(pack_kernel, groups, height, chunks),
        out_shape=pltpu.VMEM((groups * height, ROWS, width // LANES, FIELDS, LANES), density.dtype),
        in_specs=[hbm, hbm],
        out_specs=pl.BlockSpec(memory_space=pltpu.VMEM),
        scratch_shapes=[pltpu.VMEM((FIELDS,) + natural, jnp.float32), pltpu.SemaphoreType.DMA((chunks, 2))],
        cost_estimate=pl.CostEstimate(flops=0, bytes_accessed=64 * density.size, transcendentals=0),
        compiler_params=pltpu.CompilerParams(vmem_limit_bytes=12 * 2**20),
        name="pack",
    )(in_hbm(density.reshape(natural)), in_hbm(carried.reshape((FIELDS - 1,) + natural)))


def shift_kernel(blocks, tiles, chunks, height, shift_ref, fraction_ref, x_ref, o_ref, placed, out_sems):
    size = blocks // chunks
    tile_bits, skip = tiles.bit_length() - 1, (ROWS - 1) * tiles
    total = blocks * tiles
    lane = lax.broadcasted_iota(jnp.int32, (FIELDS, LANES), 1)
    base = (lax.axis_index("phi") // height) * ROWS
    shifts = [shift_ref[base + row] for row in range(ROWS)]
    whole = [s // LANES for s in shifts]
    part = [s % LANES for s in shifts]
    fraction = [fraction_ref[base + row] for row in range(ROWS)]

    def turned(row, tile):
        source = (tile - whole[row]) & (total - 1)
        return pltpu.roll(x_ref[source + (source >> tile_bits) * skip + row * tiles], part[row], 1)

    def step(tile, row, carry):
        turned_before, moved_before = carry
        now = turned(row, tile)
        first = jnp.where(lane >= part[row], now, turned_before)
        rolled = pltpu.roll(first, 1, 1)
        second = jnp.where(lane >= 1, rolled, moved_before)
        value = (1.0 - fraction[row]) * first + fraction[row] * second
        return value, (now, rolled)

    def place(block, carries):
        carries = list(carries)
        for t in range(tiles):
            for row in range(ROWS):
                placed[block, row, t], carries[row] = step(block * tiles + t, row, carries[row])
        return tuple(carries)

    carries = []
    for row in range(ROWS):
        before = turned(row, -2)
        carries.append(step(-1, row, (before, before))[1])
    carries = tuple(carries)
    departures = []
    for i in range(chunks):
        piece = pl.ds(i * size, size)
        carries = lax.fori_loop(i * size, (i + 1) * size, place, carries, unroll=4)
        departures.append(pltpu.make_async_copy(placed.at[piece], o_ref.at[piece], out_sems.at[i]))
        departures[i].start()
    for copy in departures:
        copy.wait()


def shift_rows(received, shifts, fractions, height, chunks=8):
    blocks, _, tiles, _, _ = received.shape
    smem, hbm = pl.BlockSpec(memory_space=pltpu.SMEM), pl.BlockSpec(memory_space=pltpu.HBM)
    return pl.pallas_call(
        functools.partial(shift_kernel, blocks, tiles, chunks, height),
        out_shape=pltpu.HBM(received.shape, received.dtype),
        in_specs=[smem, smem, pl.BlockSpec(memory_space=pltpu.VMEM)],
        out_specs=hbm,
        scratch_shapes=[pltpu.VMEM(received.shape, jnp.float32), pltpu.SemaphoreType.DMA((chunks,))],
        cost_estimate=pl.CostEstimate(
            flops=8 * received.size, bytes_accessed=8 * received.size, transcendentals=0
        ),
        compiler_params=pltpu.CompilerParams(vmem_limit_bytes=20 * 2**20),
        name="shift_rows",
    )(shifts, fractions, pltpu.with_memory_space_constraint(received.reshape(-1, FIELDS, LANES), pltpu.VMEM))


def edge_fluxes(height, inner, first_rows, last_rows, outer, left, first_cells, last_cells, right, rows_ref, cells_ref):
    def layer(ref, c):
        return ref[c * height : (c + 1) * height, :]

    def velocity(ref, direction):
        rho = layer(ref, 0)
        return layer(ref, 1 + direction) / jnp.where(rho == 0.0, 1.0, rho)

    def fluxes(lower, upper, direction, scale, out, start):
        v_lower, v_upper = velocity(lower, direction), velocity(upper, direction)
        speed = face_speed(v_lower, v_upper)
        for c in range(FIELDS):
            flux = flux2(v_lower, v_upper, speed, layer(lower, c), layer(upper, c))
            out[start + c * height : start + (c + 1) * height, :] = scale * flux

    fluxes(inner, first_rows, 0, 0.04, rows_ref, 0)
    fluxes(last_rows, outer, 0, -0.04, rows_ref, FIELDS * height)
    fluxes(left, first_cells, 1, 0.04, cells_ref, 0)
    fluxes(last_cells, right, 1, -0.04, cells_ref, FIELDS * height)


def finish_kernel(
    groups,
    height,
    chunks,
    moved_ref,
    near_ref,
    far_ref,
    *refs,
):
    row_refs, cell_refs = refs[:4], refs[4:8]
    density_ref, carried_ref, layer_rows, layer_cells, taken, change, edge_rows, edge_cells, new = refs[8:17]
    edge_sems, in_sems, out_sems = refs[17:]
    size = groups // chunks
    width = change.shape[-1]
    lane = lax.broadcasted_iota(jnp.int32, (ROWS, LANES), 1)
    sub = lax.broadcasted_iota(jnp.int32, (ROWS, LANES), 0)
    edges = []
    for i in range(4):
        edges.append(pltpu.make_async_copy(row_refs[i], layer_rows.at[i], edge_sems.at[0, i]))
        edges.append(pltpu.make_async_copy(cell_refs[i], layer_cells.at[i], edge_sems.at[1, i]))
    for copy in edges:
        copy.start()
    arrivals, departures = [], []
    for i in range(chunks):
        piece = pl.ds(i * size, size)
        ends = ((moved_ref.at[piece], taken.at[piece]), (far_ref.at[:, :, piece], change.at[:, :, piece]))
        arrivals.append([pltpu.make_async_copy(*pair, in_sems.at[i, k]) for k, pair in enumerate(ends)])
        for copy in arrivals[i]:
            copy.start()
    for copy in edges:
        copy.wait()
    layers = [layer_rows.at[i] for i in range(4)] + [layer_cells.at[i] for i in range(4)]
    edge_cells[2 * FIELDS * height :, :] = jnp.zeros(
        (LANES - 2 * FIELDS * height, edge_cells.shape[1]), jnp.float32
    )
    edge_fluxes(height, *layers, edge_rows, edge_cells)
    edge_cells[...] = edge_cells[...].T

    def subtract(g, _):
        cells = edge_cells[pl.ds(pl.multiple_of(g * ROWS, ROWS), ROWS), :]
        for z in range(height):
            for t in range(width // LANES):
                at = t * LANES
                by_field = exchanged([taken[g, z, row, t] for row in range(ROWS)], sub)
                for c in range(FIELDS):
                    k = c * height + z
                    by = (near_ref[c, z, g, :, at : at + LANES] if c < NEAR else change[c - NEAR, z, g, :, at : at + LANES])
                    value = by_field[c] - by
                    if at == 0:
                        value = value + jnp.where(lane == 0, cells[:, k : k + 1], 0.0)
                    if at == width - LANES:
                        m = FIELDS * height + k
                        value = value + jnp.where(lane == LANES - 1, cells[:, m : m + 1], 0.0)
                    new[c, z, g, :, at : at + LANES] = value
        return 0

    for i in range(chunks):
        piece = pl.ds(i * size, size)
        for copy in arrivals[i]:
            copy.wait()
        lax.fori_loop(i * size, (i + 1) * size, subtract, 0, unroll=4)
        for side, chunk, g, row in ((0, 0, 0, 0), (1, chunks - 1, groups - 1, ROWS - 1)):
            if i == chunk:
                for c in range(FIELDS):
                    for z in range(height):
                        k = (side * FIELDS + c) * height + z
                        here = (c, z, g, slice(row, row + 1), slice(None))
                        new[here] = new[here] + edge_rows[k : k + 1, :]
        ends = ((new.at[0, :, piece], density_ref.at[:, piece]), (new.at[1:, :, piece], carried_ref.at[:, :, piece]))
        for k, pair in enumerate(ends):
            departures.append(pltpu.make_async_copy(*pair, out_sems.at[i, k]))
            departures[-1].start()
    for copy in departures:
        copy.wait()


def finish(moved, near, far, row_layers, cell_layers, chunks=4):
    height, rows, width = near.shape[1:]
    groups = rows // ROWS
    hbm = pl.BlockSpec(memory_space=pltpu.HBM)
    natural = (height, groups, ROWS, width)
    layers = row_layers + cell_layers
    return pl.pallas_call(
        functools.partial(finish_kernel, groups, height, chunks),
        out_shape=[
            jax.ShapeDtypeStruct(natural, jnp.float32),
            jax.ShapeDtypeStruct((FIELDS - 1,) + natural, jnp.float32),
        ],
        in_specs=[hbm, pl.BlockSpec(memory_space=pltpu.VMEM), hbm] + [pl.BlockSpec(memory_space=pl.ANY)] * 8,
        out_specs=[hbm, hbm],
        scratch_shapes=[
            pltpu.VMEM((4,) + row_layers[0].shape, jnp.float32),
            pltpu.VMEM((4,) + cell_layers[0].shape, jnp.float32),
            pltpu.VMEM((groups, height) + moved.shape[1:], jnp.float32),
            pltpu.VMEM((FIELDS - NEAR,) + natural, jnp.float32),
            pltpu.VMEM((2 * FIELDS * height, width), jnp.float32),
            pltpu.VMEM((LANES, rows), jnp.float32),
            pltpu.VMEM((FIELDS,) + natural, jnp.float32),
            pltpu.SemaphoreType.DMA((2, 4)),
            pltpu.SemaphoreType.DMA((chunks, 2)),
            pltpu.SemaphoreType.DMA((chunks, 2)),
        ],
        cost_estimate=pl.CostEstimate(flops=moved.size, bytes_accessed=12 * moved.size, transcendentals=0),
        compiler_params=pltpu.CompilerParams(vmem_limit_bytes=16 * 2**20),
        name="finish",
    )(in_hbm(moved.reshape((groups, height) + moved.shape[1:])), near.reshape((NEAR,) + natural), in_hbm(far.reshape((FIELDS - NEAR,) + natural)), *layers)


def flux2(v_left, v_right, speed, q_left, q_right):
    return v_left * q_left + v_right * q_right - speed * (q_right - q_left)


def face_speed(v_left, v_right):
    return jnp.maximum(jnp.abs(v_left), jnp.abs(v_right)) + 1.0


def update_kernel(groups, width, density_ref, carried_ref, near_ref, far_ref, lower_ref):
    column = lax.broadcasted_iota(jnp.int32, (ROWS, width), 1)
    sub = lax.broadcasted_iota(jnp.int32, (ROWS, width), 0)
    lower_ref[...] = jnp.zeros_like(lower_ref)

    def field(c, z, rows):
        return density_ref[z, rows, :] if c == 0 else carried_ref[c - 1, z, rows, :]

    def body(g, _):
        rows = pl.ds(pl.multiple_of(g * ROWS, ROWS), ROWS)
        after = pl.ds(pl.multiple_of(jnp.minimum(g + 1, groups - 1) * ROWS, ROWS), ROWS)
        inside = jnp.where(g == groups - 1, ROWS - 1, ROWS)
        rho = [field(0, z, rows) for z in range(2)]
        v_height = [field(3, z, rows) / rho[z] for z in range(2)]
        speed_height = 2.0 * face_speed(v_height[0], v_height[1])
        for z in range(2):
            v_r = field(1, z, rows) / rho[z]
            v_a = field(2, z, rows) / rho[z]
            v_r_next = field(1, z, after) / field(0, z, after)
            v_r_up = pltpu.roll(jnp.where(sub == 0, v_r_next, v_r), ROWS - 1, 0)
            speed_r = face_speed(v_r, v_r_up)
            v_a_up = pltpu.roll(v_a, width - 1, 1)
            speed_a = face_speed(v_a, v_a_up)
            for c in range(FIELDS):
                q = field(c, z, rows)
                q_up = pltpu.roll(jnp.where(sub == 0, field(c, z, after), q), ROWS - 1, 0)
                upper = jnp.where(sub < inside, flux2(v_r, v_r_up, speed_r, q, q_up), 0.0)
                lower = pltpu.roll(jnp.where(sub == ROWS - 1, lower_ref[c, z], upper), 1, 0)
                lower_ref[c, z] = upper
                total = upper - lower
                q_up = pltpu.roll(q, width - 1, 1)
                upper = jnp.where(column < width - 1, flux2(v_a, v_a_up, speed_a, q, q_up), 0.0)
                total = total + (upper - pltpu.roll(upper, 1, 1))
                total = total + speed_height * (q - field(c, 1 - z, rows))
                if c < NEAR:
                    near_ref[c, z, rows, :] = 0.04 * total
                else:
                    far_ref[c - NEAR, z, rows, :] = 0.04 * total
        return 0

    lax.fori_loop(0, groups, body, 0)


def update_of(density, carried):
    rows, width = density.shape[1:]
    size = FIELDS * density.size
    vmem = pl.BlockSpec(memory_space=pltpu.VMEM)
    return pl.pallas_call(
        functools.partial(update_kernel, rows // ROWS, width),
        out_shape=[
            jax.ShapeDtypeStruct((NEAR,) + density.shape, density.dtype),
            pltpu.HBM((FIELDS - NEAR,) + density.shape, density.dtype),
        ],
        in_specs=[vmem] * 2,
        out_specs=[vmem] * 2,
        scratch_shapes=[pltpu.VMEM((FIELDS, 2, ROWS, width), jnp.float32)],
        cost_estimate=pl.CostEstimate(flops=40 * size, bytes_accessed=8 * size, transcendentals=0),
        compiler_params=pltpu.CompilerParams(vmem_limit_bytes=24 * 2**20),
        name="flux_update",
    )(density, carried)


def border_kernel(groups, height, width, density_ref, carried_ref, first_rows, last_rows, first_cells, last_cells, rows, cells, columns, sems):
    copies = []
    for side, g, at in ((0, 0, 0), (1, groups - 1, width - LANES)):
        for i, (source, fields) in enumerate(((density_ref, 0), (carried_ref, pl.ds(1, FIELDS - 1)))):
            lead = (slice(None),) * (1 + i)
            rest = (slice(None),) * 2
            copies.append(pltpu.make_async_copy(source.at[lead + (g,)], rows.at[side, fields], sems.at[side, i, 0]))
            copies.append(
                pltpu.make_async_copy(
                    source.at[lead + rest + (pl.ds(at, LANES),)], cells.at[side, fields], sems.at[side, i, 1]
                )
            )
    for copy in copies:
        copy.start()
    for copy in copies:
        copy.wait()
    lane = lax.broadcasted_iota(jnp.int32, (ROWS, LANES), 1)
    for side, out, row in ((0, first_rows, 0), (1, last_rows, ROWS - 1)):
        for k in range(FIELDS * height):
            out[k : k + 1, :] = rows[side, k // height, k % height, row : row + 1, :]

    def gather(g, _):
        here = pl.ds(pl.multiple_of(g * ROWS, ROWS), ROWS)
        for side, at in ((0, 0), (1, LANES - 1)):
            total = jnp.zeros((ROWS, LANES), jnp.float32)
            for k in range(FIELDS * height):
                value = pltpu.roll(cells[side, k // height, k % height, g], (k - at) % LANES, 1)
                total = jnp.where(lane == k, value, total)
            columns[side, here, :] = total
        return 0

    lax.fori_loop(0, groups, gather, 0)
    first_cells[...] = columns[0].T[: FIELDS * height]
    last_cells[...] = columns[1].T[: FIELDS * height]


def borders_of(density, carried):
    height, rows, width = density.shape
    groups = rows // ROWS
    natural = (height, groups, ROWS, width)
    row_shape = pltpu.HBM((FIELDS * height, width), jnp.float32)
    cell_shape = pltpu.HBM((FIELDS * height, rows), jnp.float32)
    return pl.pallas_call(
        functools.partial(border_kernel, groups, height, width),
        out_shape=[row_shape, row_shape, cell_shape, cell_shape],
        in_specs=[pl.BlockSpec(memory_space=pltpu.HBM)] * 2,
        out_specs=[pl.BlockSpec(memory_space=pltpu.VMEM)] * 4,
        scratch_shapes=[
            pltpu.VMEM((2, FIELDS, height, ROWS, width), jnp.float32),
            pltpu.VMEM((2, FIELDS, height, groups, ROWS, LANES), jnp.float32),
            pltpu.VMEM((2, rows, LANES), jnp.float32),
            pltpu.SemaphoreType.DMA((2, 2, 2)),
        ],
        compiler_params=pltpu.CompilerParams(vmem_limit_bytes=8 * 2**20),
        name="borders",
    )(in_hbm(density.reshape(natural)), in_hbm(carried.reshape((FIELDS - 1,) + natural)))


def local(density, carried, cycle_shift, cycle_fraction):
    height = density.shape[0]
    received = lax.all_to_all(pack(density, carried), "phi", 0, 0, tiled=True)
    moved = shift_rows(received, cycle_shift, cycle_fraction, height)
    moved, density, carried = lax.optimization_barrier((moved, density, carried))
    moved = lax.all_to_all(moved, "phi", 0, 0, tiled=True)

    first_rows, last_rows, first_cells, last_cells = borders_of(density, carried)
    inner = neighbours(last_rows, "rad", 1, False)
    outer = neighbours(first_rows, "rad", -1, False)
    left = neighbours(last_cells, "phi", 1, True)
    right = neighbours(first_cells, "phi", -1, True)
    near, far = update_of(density, carried)
    density_next, carried_next = finish(
        moved,
        near,
        far,
        [inner, first_rows, last_rows, outer],
        [left, first_cells, last_cells, right],
    )
    return density_next.reshape(density.shape), carried_next.reshape(carried.shape)


def solution(mesh):
    placed = (P(None, "rad", "phi"), P(None, None, "rad", "phi"), P("rad"), P("rad"))
    return jax.shard_map(
        local,
        mesh=mesh,
        in_specs=placed,
        out_specs=(P(None, "rad", "phi"), P(None, None, "rad", "phi")),
        check_vma=False,
    )
```

```python
import functools

import jax
import jax.numpy as jnp
from jax import lax
from jax.experimental import pallas as pl
from jax.experimental.pallas import tpu as pltpu
from jax.sharding import PartitionSpec as P

FIELDS = 8
ROWS = 8
LANES = 128
NEAR = 6


def neighbours(value, axis, step, wrap):
    count = lax.axis_size(axis)
    pairs = [(i, i + step) for i in range(count)]
    if wrap:
        pairs = [(i, j % count) for i, j in pairs]
    else:
        pairs = [(i, j) for i, j in pairs if 0 <= j < count]
    return lax.ppermute(value, axis, pairs)


def in_hbm(value):
    return pltpu.with_memory_space_constraint(value, pltpu.HBM)


def exchanged(registers, sub):
    values = list(registers)
    for k in (4, 2, 1):
        low = (sub & k) == 0
        result = list(values)
        for i in range(ROWS):
            if not i & k:
                a, b = values[i], values[i + k]
                result[i] = jnp.where(low, a, pltpu.roll(b, k, 0))
                result[i + k] = jnp.where(low, pltpu.roll(a, ROWS - k, 0), b)
        values = result
    return values


def pack_kernel(groups, height, chunks, density_ref, carried_ref, o_ref, taken, sems):
    size = groups // chunks
    width = taken.shape[-1]
    sub = lax.broadcasted_iota(jnp.int32, (ROWS, LANES), 0)
    arrivals = []
    for i in range(chunks):
        piece = pl.ds(i * size, size)
        ends = ((density_ref.at[:, piece], taken.at[0, :, piece]), (carried_ref.at[:, :, piece], taken.at[1:, :, piece]))
        arrivals.append([pltpu.make_async_copy(*pair, sems.at[i, k]) for k, pair in enumerate(ends)])
        for copy in arrivals[i]:
            copy.start()

    def reorder(g, _):
        for z in range(height):
            for t in range(width // LANES):
                by_row = exchanged([taken[c, z, g, :, t * LANES : (t + 1) * LANES] for c in range(FIELDS)], sub)
                for row in range(ROWS):
                    o_ref[g * height + z, row, t] = by_row[row]
        return 0

    for i in range(chunks):
        for copy in arrivals[i]:
            copy.wait()
        lax.fori_loop(i * size, (i + 1) * size, reorder, 0, unroll=2)


def pack(density, carried, chunks=4):
    height, rows, width = density.shape
    groups = rows // ROWS
    natural = (height, groups, ROWS, width)
    hbm = pl.BlockSpec(memory_space=pltpu.HBM)
    return pl.pallas_call(
        functools.partial(pack_kernel, groups, height, chunks),
        out_shape=pltpu.VMEM((groups * height, ROWS, width // LANES, FIELDS, LANES), density.dtype),
        in_specs=[hbm, hbm],
        out_specs=pl.BlockSpec(memory_space=pltpu.VMEM),
        scratch_shapes=[pltpu.VMEM((FIELDS,) + natural, jnp.float32), pltpu.SemaphoreType.DMA((chunks, 2))],
        cost_estimate=pl.CostEstimate(flops=0, bytes_accessed=64 * density.size, transcendentals=0),
        compiler_params=pltpu.CompilerParams(vmem_limit_bytes=12 * 2**20),
        name="pack",
    )(in_hbm(density.reshape(natural)), in_hbm(carried.reshape((FIELDS - 1,) + natural)))


def shift_kernel(blocks, tiles, chunks, height, shift_ref, fraction_ref, x_ref, o_ref, placed, out_sems):
    size = blocks // chunks
    tile_bits, skip = tiles.bit_length() - 1, (ROWS - 1) * tiles
    total = blocks * tiles
    lane = lax.broadcasted_iota(jnp.int32, (FIELDS, LANES), 1)
    base = (lax.axis_index("phi") // height) * ROWS
    shifts = [shift_ref[base + row] for row in range(ROWS)]
    whole = [s // LANES for s in shifts]
    part = [s % LANES for s in shifts]
    fraction = [fraction_ref[base + row] for row in range(ROWS)]

    def turned(row, tile):
        source = (tile - whole[row]) & (total - 1)
        return pltpu.roll(x_ref[source + (source >> tile_bits) * skip + row * tiles], part[row], 1)

    def step(tile, row, carry):
        turned_before, moved_before = carry
        now = turned(row, tile)
        first = jnp.where(lane >= part[row], now, turned_before)
        rolled = pltpu.roll(first, 1, 1)
        second = jnp.where(lane >= 1, rolled, moved_before)
        value = (1.0 - fraction[row]) * first + fraction[row] * second
        return value, (now, rolled)

    def place(block, carries):
        carries = list(carries)
        for t in range(tiles):
            for row in range(ROWS):
                placed[block, row, t], carries[row] = step(block * tiles + t, row, carries[row])
        return tuple(carries)

    carries = []
    for row in range(ROWS):
        before = turned(row, -2)
        carries.append(step(-1, row, (before, before))[1])
    carries = tuple(carries)
    departures = []
    for i in range(chunks):
        piece = pl.ds(i * size, size)
        carries = lax.fori_loop(i * size, (i + 1) * size, place, carries, unroll=4)
        departures.append(pltpu.make_async_copy(placed.at[piece], o_ref.at[piece], out_sems.at[i]))
        departures[i].start()
    for copy in departures:
        copy.wait()


def shift_rows(received, shifts, fractions, height, chunks=8):
    blocks, _, tiles, _, _ = received.shape
    smem, hbm = pl.BlockSpec(memory_space=pltpu.SMEM), pl.BlockSpec(memory_space=pltpu.HBM)
    return pl.pallas_call(
        functools.partial(shift_kernel, blocks, tiles, chunks, height),
        out_shape=pltpu.HBM(received.shape, received.dtype),
        in_specs=[smem, smem, pl.BlockSpec(memory_space=pltpu.VMEM)],
        out_specs=hbm,
        scratch_shapes=[pltpu.VMEM(received.shape, jnp.float32), pltpu.SemaphoreType.DMA((chunks,))],
        cost_estimate=pl.CostEstimate(
            flops=8 * received.size, bytes_accessed=8 * received.size, transcendentals=0
        ),
        compiler_params=pltpu.CompilerParams(vmem_limit_bytes=20 * 2**20),
        name="shift_rows",
    )(shifts, fractions, pltpu.with_memory_space_constraint(received.reshape(-1, FIELDS, LANES), pltpu.VMEM))


def edge_fluxes(height, inner, first_rows, last_rows, outer, left, first_cells, last_cells, right, rows_ref, cells_ref):
    def layer(ref, c):
        return ref[c * height : (c + 1) * height, :]

    def velocity(ref, direction):
        rho = layer(ref, 0)
        return layer(ref, 1 + direction) / jnp.where(rho == 0.0, 1.0, rho)

    def fluxes(lower, upper, direction, scale, out, start):
        v_lower, v_upper = velocity(lower, direction), velocity(upper, direction)
        speed = face_speed(v_lower, v_upper)
        for c in range(FIELDS):
            flux = flux2(v_lower, v_upper, speed, layer(lower, c), layer(upper, c))
            out[start + c * height : start + (c + 1) * height, :] = scale * flux

    fluxes(inner, first_rows, 0, 0.04, rows_ref, 0)
    fluxes(last_rows, outer, 0, -0.04, rows_ref, FIELDS * height)
    fluxes(left, first_cells, 1, 0.04, cells_ref, 0)
    fluxes(last_cells, right, 1, -0.04, cells_ref, FIELDS * height)


def finish_kernel(
    groups,
    height,
    chunks,
    moved_ref,
    near_ref,
    far_ref,
    *refs,
):
    density_ref, carried_ref, taken, change, edge_rows, edge_cells, new = refs[8:15]
    in_sems, out_sems = refs[15:]
    size = groups // chunks
    width = change.shape[-1]
    lane = lax.broadcasted_iota(jnp.int32, (ROWS, LANES), 1)
    sub = lax.broadcasted_iota(jnp.int32, (ROWS, LANES), 0)
    arrivals, departures = [], []
    for i in range(chunks):
        piece = pl.ds(i * size, size)
        ends = ((moved_ref.at[piece], taken.at[piece]), (far_ref.at[:, :, piece], change.at[:, :, piece]))
        arrivals.append([pltpu.make_async_copy(*pair, in_sems.at[i, k]) for k, pair in enumerate(ends)])
        for copy in arrivals[i]:
            copy.start()
    edge_cells[2 * FIELDS * height :, :] = jnp.zeros(
        (LANES - 2 * FIELDS * height, edge_cells.shape[1]), jnp.float32
    )
    edge_fluxes(height, *refs[:8], edge_rows, edge_cells)
    edge_cells[...] = edge_cells[...].T

    def subtract(g, _):
        cells = edge_cells[pl.ds(pl.multiple_of(g * ROWS, ROWS), ROWS), :]
        for z in range(height):
            for t in range(width // LANES):
                at = t * LANES
                by_field = exchanged([taken[g, z, row, t] for row in range(ROWS)], sub)
                for c in range(FIELDS):
                    k = c * height + z
                    by = (near_ref[c, z, g, :, at : at + LANES] if c < NEAR else change[c - NEAR, z, g, :, at : at + LANES])
                    value = by_field[c] - by
                    if at == 0:
                        value = value + jnp.where(lane == 0, cells[:, k : k + 1], 0.0)
                    if at == width - LANES:
                        m = FIELDS * height + k
                        value = value + jnp.where(lane == LANES - 1, cells[:, m : m + 1], 0.0)
                    new[c, z, g, :, at : at + LANES] = value
        return 0

    for i in range(chunks):
        piece = pl.ds(i * size, size)
        for copy in arrivals[i]:
            copy.wait()
        lax.fori_loop(i * size, (i + 1) * size, subtract, 0, unroll=4)
        for side, chunk, g, row in ((0, 0, 0, 0), (1, chunks - 1, groups - 1, ROWS - 1)):
            if i == chunk:
                for c in range(FIELDS):
                    for z in range(height):
                        k = (side * FIELDS + c) * height + z
                        here = (c, z, g, slice(row, row + 1), slice(None))
                        new[here] = new[here] + edge_rows[k : k + 1, :]
        ends = ((new.at[0, :, piece], density_ref.at[:, piece]), (new.at[1:, :, piece], carried_ref.at[:, :, piece]))
        for k, pair in enumerate(ends):
            departures.append(pltpu.make_async_copy(*pair, out_sems.at[i, k]))
            departures[-1].start()
    for copy in departures:
        copy.wait()


def finish(moved, near, far, row_layers, cell_layers, chunks=4):
    height, rows, width = near.shape[1:]
    groups = rows // ROWS
    hbm = pl.BlockSpec(memory_space=pltpu.HBM)
    natural = (height, groups, ROWS, width)
    layers = row_layers + cell_layers
    return pl.pallas_call(
        functools.partial(finish_kernel, groups, height, chunks),
        out_shape=[
            jax.ShapeDtypeStruct(natural, jnp.float32),
            jax.ShapeDtypeStruct((FIELDS - 1,) + natural, jnp.float32),
        ],
        in_specs=[hbm, pl.BlockSpec(memory_space=pltpu.VMEM), hbm] + [pl.BlockSpec(memory_space=pltpu.VMEM)] * 8,
        out_specs=[hbm, hbm],
        scratch_shapes=[
            pltpu.VMEM((groups, height) + moved.shape[1:], jnp.float32),
            pltpu.VMEM((FIELDS - NEAR,) + natural, jnp.float32),
            pltpu.VMEM((2 * FIELDS * height, width), jnp.float32),
            pltpu.VMEM((LANES, rows), jnp.float32),
            pltpu.VMEM((FIELDS,) + natural, jnp.float32),
            pltpu.SemaphoreType.DMA((chunks, 2)),
            pltpu.SemaphoreType.DMA((chunks, 2)),
        ],
        cost_estimate=pl.CostEstimate(flops=moved.size, bytes_accessed=12 * moved.size, transcendentals=0),
        compiler_params=pltpu.CompilerParams(vmem_limit_bytes=16 * 2**20),
        name="finish",
    )(in_hbm(moved.reshape((groups, height) + moved.shape[1:])), near.reshape((NEAR,) + natural), in_hbm(far.reshape((FIELDS - NEAR,) + natural)), *layers)


def flux2(v_left, v_right, speed, q_left, q_right):
    return v_left * q_left + v_right * q_right - speed * (q_right - q_left)


def face_speed(v_left, v_right):
    return jnp.maximum(jnp.abs(v_left), jnp.abs(v_right)) + 1.0


def update_kernel(groups, width, density_ref, carried_ref, near_ref, far_ref, lower_ref):
    column = lax.broadcasted_iota(jnp.int32, (ROWS, width), 1)
    sub = lax.broadcasted_iota(jnp.int32, (ROWS, width), 0)
    lower_ref[...] = jnp.zeros_like(lower_ref)

    def field(c, z, rows):
        return density_ref[z, rows, :] if c == 0 else carried_ref[c - 1, z, rows, :]

    def body(g, _):
        rows = pl.ds(pl.multiple_of(g * ROWS, ROWS), ROWS)
        after = pl.ds(pl.multiple_of(jnp.minimum(g + 1, groups - 1) * ROWS, ROWS), ROWS)
        inside = jnp.where(g == groups - 1, ROWS - 1, ROWS)
        rho = [field(0, z, rows) for z in range(2)]
        v_height = [field(3, z, rows) / rho[z] for z in range(2)]
        speed_height = 2.0 * face_speed(v_height[0], v_height[1])
        for z in range(2):
            v_r = field(1, z, rows) / rho[z]
            v_a = field(2, z, rows) / rho[z]
            v_r_next = field(1, z, after) / field(0, z, after)
            v_r_up = pltpu.roll(jnp.where(sub == 0, v_r_next, v_r), ROWS - 1, 0)
            speed_r = face_speed(v_r, v_r_up)
            v_a_up = pltpu.roll(v_a, width - 1, 1)
            speed_a = face_speed(v_a, v_a_up)
            for c in range(FIELDS):
                q = field(c, z, rows)
                q_up = pltpu.roll(jnp.where(sub == 0, field(c, z, after), q), ROWS - 1, 0)
                upper = jnp.where(sub < inside, flux2(v_r, v_r_up, speed_r, q, q_up), 0.0)
                lower = pltpu.roll(jnp.where(sub == ROWS - 1, lower_ref[c, z], upper), 1, 0)
                lower_ref[c, z] = upper
                total = upper - lower
                q_up = pltpu.roll(q, width - 1, 1)
                upper = jnp.where(column < width - 1, flux2(v_a, v_a_up, speed_a, q, q_up), 0.0)
                total = total + (upper - pltpu.roll(upper, 1, 1))
                total = total + speed_height * (q - field(c, 1 - z, rows))
                if c < NEAR:
                    near_ref[c, z, rows, :] = 0.04 * total
                else:
                    far_ref[c - NEAR, z, rows, :] = 0.04 * total
        return 0

    lax.fori_loop(0, groups, body, 0)


def update_of(density, carried):
    rows, width = density.shape[1:]
    size = FIELDS * density.size
    vmem = pl.BlockSpec(memory_space=pltpu.VMEM)
    return pl.pallas_call(
        functools.partial(update_kernel, rows // ROWS, width),
        out_shape=[
            jax.ShapeDtypeStruct((NEAR,) + density.shape, density.dtype),
            pltpu.HBM((FIELDS - NEAR,) + density.shape, density.dtype),
        ],
        in_specs=[vmem] * 2,
        out_specs=[vmem] * 2,
        scratch_shapes=[pltpu.VMEM((FIELDS, 2, ROWS, width), jnp.float32)],
        cost_estimate=pl.CostEstimate(flops=40 * size, bytes_accessed=8 * size, transcendentals=0),
        compiler_params=pltpu.CompilerParams(vmem_limit_bytes=24 * 2**20),
        name="flux_update",
    )(density, carried)


def border_kernel(groups, height, width, density_ref, carried_ref, first_rows, last_rows, first_cells, last_cells, rows, cells, columns, sems):
    copies = []
    for side, g, at in ((0, 0, 0), (1, groups - 1, width - LANES)):
        for i, (source, fields) in enumerate(((density_ref, 0), (carried_ref, pl.ds(1, FIELDS - 1)))):
            lead = (slice(None),) * (1 + i)
            rest = (slice(None),) * 2
            copies.append(pltpu.make_async_copy(source.at[lead + (g,)], rows.at[side, fields], sems.at[side, i, 0]))
            copies.append(
                pltpu.make_async_copy(
                    source.at[lead + rest + (pl.ds(at, LANES),)], cells.at[side, fields], sems.at[side, i, 1]
                )
            )
    for copy in copies:
        copy.start()
    for copy in copies:
        copy.wait()
    lane = lax.broadcasted_iota(jnp.int32, (ROWS, LANES), 1)
    for side, out, row in ((0, first_rows, 0), (1, last_rows, ROWS - 1)):
        for k in range(FIELDS * height):
            out[k : k + 1, :] = rows[side, k // height, k % height, row : row + 1, :]

    def gather(g, _):
        here = pl.ds(pl.multiple_of(g * ROWS, ROWS), ROWS)
        for side, at in ((0, 0), (1, LANES - 1)):
            total = jnp.zeros((ROWS, LANES), jnp.float32)
            for k in range(FIELDS * height):
                value = pltpu.roll(cells[side, k // height, k % height, g], (k - at) % LANES, 1)
                total = jnp.where(lane == k, value, total)
            columns[side, here, :] = total
        return 0

    lax.fori_loop(0, groups, gather, 0)
    first_cells[...] = columns[0].T[: FIELDS * height]
    last_cells[...] = columns[1].T[: FIELDS * height]


def borders_of(density, carried):
    height, rows, width = density.shape
    groups = rows // ROWS
    natural = (height, groups, ROWS, width)
    row_shape = pltpu.HBM((FIELDS * height, width), jnp.float32)
    cell_shape = pltpu.HBM((FIELDS * height, rows), jnp.float32)
    return pl.pallas_call(
        functools.partial(border_kernel, groups, height, width),
        out_shape=[row_shape, row_shape, cell_shape, cell_shape],
        in_specs=[pl.BlockSpec(memory_space=pltpu.HBM)] * 2,
        out_specs=[pl.BlockSpec(memory_space=pltpu.VMEM)] * 4,
        scratch_shapes=[
            pltpu.VMEM((2, FIELDS, height, ROWS, width), jnp.float32),
            pltpu.VMEM((2, FIELDS, height, groups, ROWS, LANES), jnp.float32),
            pltpu.VMEM((2, rows, LANES), jnp.float32),
            pltpu.SemaphoreType.DMA((2, 2, 2)),
        ],
        compiler_params=pltpu.CompilerParams(vmem_limit_bytes=8 * 2**20),
        name="borders",
    )(in_hbm(density.reshape(natural)), in_hbm(carried.reshape((FIELDS - 1,) + natural)))


def local(density, carried, cycle_shift, cycle_fraction):
    height = density.shape[0]
    received = lax.all_to_all(pack(density, carried), "phi", 0, 0, tiled=True)
    moved = shift_rows(received, cycle_shift, cycle_fraction, height)
    moved, density, carried = lax.optimization_barrier((moved, density, carried))
    moved = lax.all_to_all(moved, "phi", 0, 0, tiled=True)

    first_rows, last_rows, first_cells, last_cells = borders_of(density, carried)
    inner = neighbours(last_rows, "rad", 1, False)
    outer = neighbours(first_rows, "rad", -1, False)
    left = neighbours(last_cells, "phi", 1, True)
    right = neighbours(first_cells, "phi", -1, True)
    near, far = update_of(density, carried)
    density_next, carried_next = finish(
        moved,
        near,
        far,
        [inner, first_rows, last_rows, outer],
        [left, first_cells, last_cells, right],
    )
    return density_next.reshape(density.shape), carried_next.reshape(carried.shape)


def solution(mesh):
    placed = (P(None, "rad", "phi"), P(None, None, "rad", "phi"), P("rad"), P("rad"))
    return jax.shard_map(
        local,
        mesh=mesh,
        in_specs=placed,
        out_specs=(P(None, "rad", "phi"), P(None, None, "rad", "phi")),
        check_vma=False,
    )
```

```python
import functools

import jax
import jax.numpy as jnp
from jax import lax
from jax.experimental import pallas as pl
from jax.experimental.pallas import tpu as pltpu
from jax.sharding import PartitionSpec as P

FIELDS = 8
ROWS = 8
LANES = 128
NEAR = 6


def neighbours(value, axis, step, wrap):
    count = lax.axis_size(axis)
    pairs = [(i, i + step) for i in range(count)]
    if wrap:
        pairs = [(i, j % count) for i, j in pairs]
    else:
        pairs = [(i, j) for i, j in pairs if 0 <= j < count]
    return lax.ppermute(value, axis, pairs)


def in_hbm(value):
    return pltpu.with_memory_space_constraint(value, pltpu.HBM)


def exchanged(registers, sub):
    values = list(registers)
    for k in (4, 2, 1):
        low = (sub & k) == 0
        result = list(values)
        for i in range(ROWS):
            if not i & k:
                a, b = values[i], values[i + k]
                result[i] = jnp.where(low, a, pltpu.roll(b, k, 0))
                result[i + k] = jnp.where(low, pltpu.roll(a, ROWS - k, 0), b)
        values = result
    return values


def pack_kernel(groups, height, chunks, density_ref, carried_ref, o_ref, taken, sems):
    size = groups // chunks
    width = taken.shape[-1]
    sub = lax.broadcasted_iota(jnp.int32, (ROWS, LANES), 0)
    arrivals = []
    for i in range(chunks):
        piece = pl.ds(i * size, size)
        ends = ((density_ref.at[:, piece], taken.at[0, :, piece]), (carried_ref.at[:, :, piece], taken.at[1:, :, piece]))
        arrivals.append([pltpu.make_async_copy(*pair, sems.at[i, k]) for k, pair in enumerate(ends)])
        for copy in arrivals[i]:
            copy.start()

    def reorder(g, _):
        for z in range(height):
            for t in range(width // LANES):
                by_row = exchanged([taken[c, z, g, :, t * LANES : (t + 1) * LANES] for c in range(FIELDS)], sub)
                for row in range(ROWS):
                    o_ref[g * height + z, row, t] = by_row[row]
        return 0

    for i in range(chunks):
        for copy in arrivals[i]:
            copy.wait()
        lax.fori_loop(i * size, (i + 1) * size, reorder, 0, unroll=1)


def pack(density, carried, chunks=8):
    height, rows, width = density.shape
    groups = rows // ROWS
    natural = (height, groups, ROWS, width)
    hbm = pl.BlockSpec(memory_space=pltpu.HBM)
    return pl.pallas_call(
        functools.partial(pack_kernel, groups, height, chunks),
        out_shape=pltpu.VMEM((groups * height, ROWS, width // LANES, FIELDS, LANES), density.dtype),
        in_specs=[hbm, hbm],
        out_specs=pl.BlockSpec(memory_space=pltpu.VMEM),
        scratch_shapes=[pltpu.VMEM((FIELDS,) + natural, jnp.float32), pltpu.SemaphoreType.DMA((chunks, 2))],
        cost_estimate=pl.CostEstimate(flops=0, bytes_accessed=64 * density.size, transcendentals=0),
        compiler_params=pltpu.CompilerParams(vmem_limit_bytes=12 * 2**20),
        name="pack",
    )(in_hbm(density.reshape(natural)), in_hbm(carried.reshape((FIELDS - 1,) + natural)))


def shift_kernel(blocks, tiles, chunks, height, shift_ref, fraction_ref, x_ref, o_ref, placed, out_sems):
    size = blocks // chunks
    tile_bits, skip = tiles.bit_length() - 1, (ROWS - 1) * tiles
    total = blocks * tiles
    lane = lax.broadcasted_iota(jnp.int32, (FIELDS, LANES), 1)
    base = (lax.axis_index("phi") // height) * ROWS
    shifts = [shift_ref[base + row] for row in range(ROWS)]
    whole = [s // LANES for s in shifts]
    part = [s % LANES for s in shifts]
    fraction = [fraction_ref[base + row] for row in range(ROWS)]

    def turned(row, tile):
        source = (tile - whole[row]) & (total - 1)
        return pltpu.roll(x_ref[source + (source >> tile_bits) * skip + row * tiles], part[row], 1)

    def step(tile, row, carry):
        turned_before, moved_before = carry
        now = turned(row, tile)
        first = jnp.where(lane >= part[row], now, turned_before)
        rolled = pltpu.roll(first, 1, 1)
        second = jnp.where(lane >= 1, rolled, moved_before)
        value = (1.0 - fraction[row]) * first + fraction[row] * second
        return value, (now, rolled)

    def place(block, carries):
        carries = list(carries)
        for t in range(tiles):
            for row in range(ROWS):
                placed[block, row, t], carries[row] = step(block * tiles + t, row, carries[row])
        return tuple(carries)

    carries = []
    for row in range(ROWS):
        before = turned(row, -2)
        carries.append(step(-1, row, (before, before))[1])
    carries = tuple(carries)
    departures = []
    for i in range(chunks):
        piece = pl.ds(i * size, size)
        carries = lax.fori_loop(i * size, (i + 1) * size, place, carries, unroll=4)
        departures.append(pltpu.make_async_copy(placed.at[piece], o_ref.at[piece], out_sems.at[i]))
        departures[i].start()
    for copy in departures:
        copy.wait()


def shift_rows(received, shifts, fractions, height, chunks=8):
    blocks, _, tiles, _, _ = received.shape
    smem, hbm = pl.BlockSpec(memory_space=pltpu.SMEM), pl.BlockSpec(memory_space=pltpu.HBM)
    return pl.pallas_call(
        functools.partial(shift_kernel, blocks, tiles, chunks, height),
        out_shape=pltpu.HBM(received.shape, received.dtype),
        in_specs=[smem, smem, pl.BlockSpec(memory_space=pltpu.VMEM)],
        out_specs=hbm,
        scratch_shapes=[pltpu.VMEM(received.shape, jnp.float32), pltpu.SemaphoreType.DMA((chunks,))],
        cost_estimate=pl.CostEstimate(
            flops=8 * received.size, bytes_accessed=8 * received.size, transcendentals=0
        ),
        compiler_params=pltpu.CompilerParams(vmem_limit_bytes=20 * 2**20),
        name="shift_rows",
    )(shifts, fractions, pltpu.with_memory_space_constraint(received.reshape(-1, FIELDS, LANES), pltpu.VMEM))


def edge_fluxes(height, inner, first_rows, last_rows, outer, left, first_cells, last_cells, right, rows_ref, cells_ref):
    def layer(ref, c):
        return ref[c * height : (c + 1) * height, :]

    def velocity(ref, direction):
        rho = layer(ref, 0)
        return layer(ref, 1 + direction) / jnp.where(rho == 0.0, 1.0, rho)

    def fluxes(lower, upper, direction, scale, out, start):
        v_lower, v_upper = velocity(lower, direction), velocity(upper, direction)
        speed = face_speed(v_lower, v_upper)
        for c in range(FIELDS):
            flux = flux2(v_lower, v_upper, speed, layer(lower, c), layer(upper, c))
            out[start + c * height : start + (c + 1) * height, :] = scale * flux

    fluxes(inner, first_rows, 0, 0.04, rows_ref, 0)
    fluxes(last_rows, outer, 0, -0.04, rows_ref, FIELDS * height)
    fluxes(left, first_cells, 1, 0.04, cells_ref, 0)
    fluxes(last_cells, right, 1, -0.04, cells_ref, FIELDS * height)


def finish_kernel(
    groups,
    height,
    chunks,
    moved_ref,
    near_ref,
    far_ref,
    *refs,
):
    density_ref, carried_ref, taken, change, edge_rows, edge_cells, new = refs[8:15]
    in_sems, out_sems = refs[15:]
    size = groups // chunks
    width = change.shape[-1]
    lane = lax.broadcasted_iota(jnp.int32, (ROWS, LANES), 1)
    sub = lax.broadcasted_iota(jnp.int32, (ROWS, LANES), 0)
    arrivals, departures = [], []
    for i in range(chunks):
        piece = pl.ds(i * size, size)
        ends = ((moved_ref.at[piece], taken.at[piece]), (far_ref.at[:, :, piece], change.at[:, :, piece]))
        arrivals.append([pltpu.make_async_copy(*pair, in_sems.at[i, k]) for k, pair in enumerate(ends)])
        for copy in arrivals[i]:
            copy.start()
    edge_cells[2 * FIELDS * height :, :] = jnp.zeros(
        (LANES - 2 * FIELDS * height, edge_cells.shape[1]), jnp.float32
    )
    edge_fluxes(height, *refs[:8], edge_rows, edge_cells)
    edge_cells[...] = edge_cells[...].T

    def subtract(g, _):
        cells = edge_cells[pl.ds(pl.multiple_of(g * ROWS, ROWS), ROWS), :]
        for z in range(height):
            for t in range(width // LANES):
                at = t * LANES
                by_field = exchanged([taken[g, z, row, t] for row in range(ROWS)], sub)
                for c in range(FIELDS):
                    k = c * height + z
                    by = (near_ref[c, z, g, :, at : at + LANES] if c < NEAR else change[c - NEAR, z, g, :, at : at + LANES])
                    value = by_field[c] - by
                    if at == 0:
                        value = value + jnp.where(lane == 0, cells[:, k : k + 1], 0.0)
                    if at == width - LANES:
                        m = FIELDS * height + k
                        value = value + jnp.where(lane == LANES - 1, cells[:, m : m + 1], 0.0)
                    new[c, z, g, :, at : at + LANES] = value
        return 0

    for i in range(chunks):
        piece = pl.ds(i * size, size)
        for copy in arrivals[i]:
            copy.wait()
        lax.fori_loop(i * size, (i + 1) * size, subtract, 0, unroll=4)
        for side, chunk, g, row in ((0, 0, 0, 0), (1, chunks - 1, groups - 1, ROWS - 1)):
            if i == chunk:
                for c in range(FIELDS):
                    for z in range(height):
                        k = (side * FIELDS + c) * height + z
                        here = (c, z, g, slice(row, row + 1), slice(None))
                        new[here] = new[here] + edge_rows[k : k + 1, :]
        ends = ((new.at[0, :, piece], density_ref.at[:, piece]), (new.at[1:, :, piece], carried_ref.at[:, :, piece]))
        for k, pair in enumerate(ends):
            departures.append(pltpu.make_async_copy(*pair, out_sems.at[i, k]))
            departures[-1].start()
    for copy in departures:
        copy.wait()


def finish(moved, near, far, row_layers, cell_layers, chunks=4):
    height, rows, width = near.shape[1:]
    groups = rows // ROWS
    hbm = pl.BlockSpec(memory_space=pltpu.HBM)
    natural = (height, groups, ROWS, width)
    layers = row_layers + cell_layers
    return pl.pallas_call(
        functools.partial(finish_kernel, groups, height, chunks),
        out_shape=[
            jax.ShapeDtypeStruct(natural, jnp.float32),
            jax.ShapeDtypeStruct((FIELDS - 1,) + natural, jnp.float32),
        ],
        in_specs=[hbm, pl.BlockSpec(memory_space=pltpu.VMEM), hbm] + [pl.BlockSpec(memory_space=pltpu.VMEM)] * 8,
        out_specs=[hbm, hbm],
        scratch_shapes=[
            pltpu.VMEM((groups, height) + moved.shape[1:], jnp.float32),
            pltpu.VMEM((FIELDS - NEAR,) + natural, jnp.float32),
            pltpu.VMEM((2 * FIELDS * height, width), jnp.float32),
            pltpu.VMEM((LANES, rows), jnp.float32),
            pltpu.VMEM((FIELDS,) + natural, jnp.float32),
            pltpu.SemaphoreType.DMA((chunks, 2)),
            pltpu.SemaphoreType.DMA((chunks, 2)),
        ],
        cost_estimate=pl.CostEstimate(flops=moved.size, bytes_accessed=12 * moved.size, transcendentals=0),
        compiler_params=pltpu.CompilerParams(vmem_limit_bytes=16 * 2**20),
        name="finish",
    )(in_hbm(moved.reshape((groups, height) + moved.shape[1:])), near.reshape((NEAR,) + natural), in_hbm(far.reshape((FIELDS - NEAR,) + natural)), *layers)


def flux2(v_left, v_right, speed, q_left, q_right):
    return v_left * q_left + v_right * q_right - speed * (q_right - q_left)


def face_speed(v_left, v_right):
    return jnp.maximum(jnp.abs(v_left), jnp.abs(v_right)) + 1.0


def update_kernel(groups, width, density_ref, carried_ref, near_ref, far_ref, lower_ref):
    column = lax.broadcasted_iota(jnp.int32, (ROWS, width), 1)
    sub = lax.broadcasted_iota(jnp.int32, (ROWS, width), 0)
    lower_ref[...] = jnp.zeros_like(lower_ref)

    def field(c, z, rows):
        return density_ref[z, rows, :] if c == 0 else carried_ref[c - 1, z, rows, :]

    def body(g, _):
        rows = pl.ds(pl.multiple_of(g * ROWS, ROWS), ROWS)
        after = pl.ds(pl.multiple_of(jnp.minimum(g + 1, groups - 1) * ROWS, ROWS), ROWS)
        inside = jnp.where(g == groups - 1, ROWS - 1, ROWS)
        rho = [field(0, z, rows) for z in range(2)]
        v_height = [field(3, z, rows) / rho[z] for z in range(2)]
        speed_height = 2.0 * face_speed(v_height[0], v_height[1])
        for z in range(2):
            v_r = field(1, z, rows) / rho[z]
            v_a = field(2, z, rows) / rho[z]
            v_r_next = field(1, z, after) / field(0, z, after)
            v_r_up = pltpu.roll(jnp.where(sub == 0, v_r_next, v_r), ROWS - 1, 0)
            speed_r = face_speed(v_r, v_r_up)
            v_a_up = pltpu.roll(v_a, width - 1, 1)
            speed_a = face_speed(v_a, v_a_up)
            for c in range(FIELDS):
                q = field(c, z, rows)
                q_up = pltpu.roll(jnp.where(sub == 0, field(c, z, after), q), ROWS - 1, 0)
                upper = jnp.where(sub < inside, flux2(v_r, v_r_up, speed_r, q, q_up), 0.0)
                lower = pltpu.roll(jnp.where(sub == ROWS - 1, lower_ref[c, z], upper), 1, 0)
                lower_ref[c, z] = upper
                total = upper - lower
                q_up = pltpu.roll(q, width - 1, 1)
                upper = jnp.where(column < width - 1, flux2(v_a, v_a_up, speed_a, q, q_up), 0.0)
                total = total + (upper - pltpu.roll(upper, 1, 1))
                total = total + speed_height * (q - field(c, 1 - z, rows))
                if c < NEAR:
                    near_ref[c, z, rows, :] = 0.04 * total
                else:
                    far_ref[c - NEAR, z, rows, :] = 0.04 * total
        return 0

    lax.fori_loop(0, groups, body, 0)


def update_of(density, carried):
    rows, width = density.shape[1:]
    size = FIELDS * density.size
    vmem = pl.BlockSpec(memory_space=pltpu.VMEM)
    return pl.pallas_call(
        functools.partial(update_kernel, rows // ROWS, width),
        out_shape=[
            jax.ShapeDtypeStruct((NEAR,) + density.shape, density.dtype),
            pltpu.HBM((FIELDS - NEAR,) + density.shape, density.dtype),
        ],
        in_specs=[vmem] * 2,
        out_specs=[vmem] * 2,
        scratch_shapes=[pltpu.VMEM((FIELDS, 2, ROWS, width), jnp.float32)],
        cost_estimate=pl.CostEstimate(flops=40 * size, bytes_accessed=8 * size, transcendentals=0),
        compiler_params=pltpu.CompilerParams(vmem_limit_bytes=24 * 2**20),
        name="flux_update",
    )(density, carried)


def border_kernel(groups, height, width, density_ref, carried_ref, first_rows, last_rows, first_cells, last_cells, rows, cells, columns, sems):
    copies = []
    for side, g, at in ((0, 0, 0), (1, groups - 1, width - LANES)):
        for i, (source, fields) in enumerate(((density_ref, 0), (carried_ref, pl.ds(1, FIELDS - 1)))):
            lead = (slice(None),) * (1 + i)
            rest = (slice(None),) * 2
            copies.append(pltpu.make_async_copy(source.at[lead + (g,)], rows.at[side, fields], sems.at[side, i, 0]))
            copies.append(
                pltpu.make_async_copy(
                    source.at[lead + rest + (pl.ds(at, LANES),)], cells.at[side, fields], sems.at[side, i, 1]
                )
            )
    for copy in copies:
        copy.start()
    for copy in copies:
        copy.wait()
    lane = lax.broadcasted_iota(jnp.int32, (ROWS, LANES), 1)
    for side, out, row in ((0, first_rows, 0), (1, last_rows, ROWS - 1)):
        for k in range(FIELDS * height):
            out[k : k + 1, :] = rows[side, k // height, k % height, row : row + 1, :]

    def gather(g, _):
        here = pl.ds(pl.multiple_of(g * ROWS, ROWS), ROWS)
        for side, at in ((0, 0), (1, LANES - 1)):
            total = jnp.zeros((ROWS, LANES), jnp.float32)
            for k in range(FIELDS * height):
                value = pltpu.roll(cells[side, k // height, k % height, g], (k - at) % LANES, 1)
                total = jnp.where(lane == k, value, total)
            columns[side, here, :] = total
        return 0

    lax.fori_loop(0, groups, gather, 0)
    first_cells[...] = columns[0].T[: FIELDS * height]
    last_cells[...] = columns[1].T[: FIELDS * height]


def borders_of(density, carried):
    height, rows, width = density.shape
    groups = rows // ROWS
    natural = (height, groups, ROWS, width)
    row_shape = pltpu.HBM((FIELDS * height, width), jnp.float32)
    cell_shape = pltpu.HBM((FIELDS * height, rows), jnp.float32)
    return pl.pallas_call(
        functools.partial(border_kernel, groups, height, width),
        out_shape=[row_shape, row_shape, cell_shape, cell_shape],
        in_specs=[pl.BlockSpec(memory_space=pltpu.HBM)] * 2,
        out_specs=[pl.BlockSpec(memory_space=pltpu.VMEM)] * 4,
        scratch_shapes=[
            pltpu.VMEM((2, FIELDS, height, ROWS, width), jnp.float32),
            pltpu.VMEM((2, FIELDS, height, groups, ROWS, LANES), jnp.float32),
            pltpu.VMEM((2, rows, LANES), jnp.float32),
            pltpu.SemaphoreType.DMA((2, 2, 2)),
        ],
        compiler_params=pltpu.CompilerParams(vmem_limit_bytes=8 * 2**20),
        name="borders",
    )(in_hbm(density.reshape(natural)), in_hbm(carried.reshape((FIELDS - 1,) + natural)))


def local(density, carried, cycle_shift, cycle_fraction):
    height = density.shape[0]
    received = lax.all_to_all(pack(density, carried), "phi", 0, 0, tiled=True)
    moved = shift_rows(received, cycle_shift, cycle_fraction, height)
    moved, density, carried = lax.optimization_barrier((moved, density, carried))
    moved = lax.all_to_all(moved, "phi", 0, 0, tiled=True)

    first_rows, last_rows, first_cells, last_cells = borders_of(density, carried)
    inner = neighbours(last_rows, "rad", 1, False)
    outer = neighbours(first_rows, "rad", -1, False)
    left = neighbours(last_cells, "phi", 1, True)
    right = neighbours(first_cells, "phi", -1, True)
    near, far = update_of(density, carried)
    density_next, carried_next = finish(
        moved,
        near,
        far,
        [inner, first_rows, last_rows, outer],
        [left, first_cells, last_cells, right],
    )
    return density_next.reshape(density.shape), carried_next.reshape(carried.shape)


def solution(mesh):
    placed = (P(None, "rad", "phi"), P(None, None, "rad", "phi"), P("rad"), P("rad"))
    return jax.shard_map(
        local,
        mesh=mesh,
        in_specs=placed,
        out_specs=(P(None, "rad", "phi"), P(None, None, "rad", "phi")),
        check_vma=False,
    )
```
